512 devices in a mesh: wide: 32 (over y, x), narrow: 16 (over z, core).
Axes of the slice: x: 4, y: 8, z: 8, core: 2. Of those that a mesh axis runs over, the one named last changes fastest.
Arguments:
- queries: bfloat16 [65536, 768], P(('wide', 'narrow')), may hold values from -8 to 8
- keys: bfloat16 [65536, 768], P(('wide', 'narrow')), may hold values from -8 to 8
- values: bfloat16 [65536, 768], P(('wide', 'narrow')), may hold values from -6 to 6
- slide_ids: int32 [65536], P(('wide', 'narrow')), may hold values from 0 to 15, never falling along the last dimension, each value on 1 to 12288 neighbouring positions
- w_out: bfloat16 [768, 768], replicated, may hold values from -0.21875 to 0.21875
Outputs:
- encoded: bfloat16 [65536, 768], P(('wide', 'narrow'))
The draws below stay inside these ranges and needn't reach their ends.
Inputs may be any that keep to these rules, and one draw needn't show every extreme that they name: `slide_ids`: slide numbers never fall along the tokens; each slide holds 1 to 12288 tokens, one exactly 12288.
All inputs are finite; a program needn't handle non-finite values.
Results may differ from the reference program's by a relative error of at most 0.0055.
Values may be sent and summed in bfloat16 or wider, within the bound.
A program may use at most 64 MiB of HBM per device.

```python
import math
from functools import reduce
import jax
import jax.numpy as jnp
import numpy as np
from jax import lax

HEADS = 12
HDIM = 64
D = 768
TOK_DEV = 128
RATE_NEAR = 4
RATE_FAR = 8
TOKENS = 65536
GROUP_TOK = 2048
SEG_FAR = 65536
NEAR_GROUPS = 8
FAR_GROUPS = 32
SLIDES = 16
MOST_SLIDE = 12288
N_NARROW = 16


def base_rows(key, salt):
    noise_key = jax.random.fold_in(key, salt)
    source = jnp.clip(jax.random.normal(noise_key, (TOKENS, HEADS, HDIM), jnp.float32), -4.0, 4.0)
    return source


def draw_queries(key, part):
    source = base_rows(key, 1)
    return source.reshape(TOKENS, HEADS * HDIM).astype(jnp.bfloat16)


def draw_keys(key, part):
    source = base_rows(key, 2)
    return source.reshape(TOKENS, HEADS * HDIM).astype(jnp.bfloat16)


def levels(key, extent, split, low, largest):
    level = 1.0
    for axis_at, blocks in split:
        draws = jax.random.uniform(jax.random.fold_in(jax.random.fold_in(key, 6), axis_at), (blocks,), jnp.float32, low / len(split), largest / len(split))
        level = level * jnp.repeat(jnp.exp(draws), extent[axis_at] // blocks).reshape((-1,) + (1,) * (len(extent) - 1 - axis_at))
    return level


def split_up(number_of, total, reach, slope):
    loads = [(1 << 20) // math.isqrt(grade ** slope) + 1 for grade in range(2, number_of + 1)]
    spare, given = total - reach - (number_of - 1), [1] * (number_of - 1)
    while spare > 0:
        movable = [i for i in range(number_of - 1) if given[i] < reach]
        pool, budget = sum([loads[i] for i in movable]), spare
        for i in movable:
            more = min(reach - given[i], max(1, budget * loads[i] // pool), spare)
            given[i] = given[i] + more
            spare = spare - more
    return np.array([reach] + given)


def ragged_sizes(stream_key, number_of, total, most, skew):
    if number_of == 2:
        one = jax.random.randint(stream_key, (), max(1, total - most), min(most, total - 1) + 1)
        return jnp.stack([one, total - one])
    sizes = jnp.asarray(split_up(number_of, total, most, skew), jnp.int32)
    pairs = (number_of - 1) // 2
    giver, sink = sizes[1:1 + 2 * pairs:2], sizes[2:2 + 2 * pairs:2]
    room = jnp.minimum(giver - 1, most - sink)
    moved = jax.random.randint(jax.random.fold_in(stream_key, 1), (pairs,), 0, 1 << 20) % (room + 1)
    sizes = sizes.at[1:1 + 2 * pairs:2].set(giver - moved).at[2:2 + 2 * pairs:2].set(sink + moved)
    return sizes[jax.random.permutation(jax.random.fold_in(stream_key, 2), number_of)]


def gaussian(key, extent, width, reach, split=(), kind=jnp.bfloat16):
    values = width * jax.random.normal(key, extent, jnp.float32)
    if split:
        values = values * levels(key, extent, split, -0.22, 0.18)
    return jnp.clip(values, -reach, reach).astype(kind)


def setup_inputs(seed: int = 0) -> dict:
    arg_keys = jax.random.split(jax.random.key(seed), 6)
    queries = draw_queries(jax.random.fold_in(arg_keys[5], 71), 0)
    keys = draw_keys(jax.random.fold_in(arg_keys[5], 71), 0)
    values = gaussian(arg_keys[2], (TOKENS, D), 1.0, 6.0, ((0, 512),))
    slide_ids = jnp.searchsorted(jnp.cumsum(ragged_sizes(arg_keys[3], SLIDES, TOKENS, MOST_SLIDE, 2)), jnp.arange(TOKENS), side="right").astype(jnp.int32)
    w_out = gaussian(arg_keys[4], (D, D), D ** -0.5, 0.21875)
    return {"queries": queries, "keys": keys, "values": values, "slide_ids": slide_ids, "w_out": w_out}


NEG_FILL = -1e30


def pick(source, dilation):
    length = source.shape[0]
    head_ids = jnp.arange(HEADS)
    return source.reshape(length // dilation, dilation, HEADS, HDIM)[:, head_ids % dilation, head_ids, :]


def pick_ids(slide_rows, dilation):
    length = slide_rows.shape[0]
    head_ids = jnp.arange(HEADS)
    return slide_rows.reshape(length // dilation, dilation)[:, head_ids % dilation]


def attend(query_rows, query_ids, key_rows, value_rows, key_ids):
    scores = jnp.einsum('qhd,khd->hqk', query_rows.astype(jnp.float32), key_rows.astype(jnp.float32)) * (HDIM ** -0.5)
    same = query_ids.T[:, :, None] == key_ids.T[:, None, :]
    scores = jnp.where(same, scores, NEG_FILL)
    maxima = jnp.max(scores, axis=-1)
    weights = jnp.where(same, jnp.exp(scores - maxima[..., None]), 0.0)
    totals = jnp.sum(weights, axis=-1)
    rounded = lax.optimization_barrier(weights.astype(jnp.bfloat16))
    summed = jnp.einsum('hqk,khd->qhd', rounded.astype(jnp.float32), value_rows.astype(jnp.float32))
    return maxima.T, totals.T, summed


def spread(part, dilation):
    head_ids = jnp.arange(HEADS)
    result = []
    for member, filler in zip(part, (NEG_FILL, 0.0, 0.0)):
        filled = jnp.full((member.shape[0], dilation) + member.shape[1:], filler, member.dtype)
        filled = filled.at[:, head_ids % dilation, head_ids].set(member)
        result.append(filled.reshape((member.shape[0] * dilation,) + member.shape[1:]))
    return tuple(result)


def combine(parts):
    top = reduce(jnp.maximum, [member[0] for member in parts])
    totals = reduce(jnp.add, [member[1] * jnp.exp(member[0] - top) for member in parts])
    numer = reduce(jnp.add, [member[2] * jnp.exp(member[0] - top)[..., None] for member in parts])
    return (numer / totals[..., None]).reshape(numer.shape[0], -1).astype(jnp.bfloat16)


def local_block(block_ops):
    query_blk, key_blk, value_blk, slide_blk = block_ops
    slide_cols = pick_ids(slide_blk, 1)
    return attend(pick(query_blk, 1), slide_cols, pick(key_blk, 1), pick(value_blk, 1), slide_cols)


def reference(queries, keys, values, slide_ids, w_out):
    segs = TOKENS // SEG_FAR

    def segment(operands):
        query_seg, key_seg, value_seg, slide_seg = operands
        near_k = jnp.stack([pick(key_seg[g], RATE_NEAR) for g in range(FAR_GROUPS)])
        near_v = jnp.stack([pick(value_seg[g], RATE_NEAR) for g in range(FAR_GROUPS)])
        near_s = jnp.stack([pick_ids(slide_seg[g], RATE_NEAR) for g in range(FAR_GROUPS)])
        far_k = [pick(key_seg[g], RATE_FAR) for g in range(FAR_GROUPS)]
        far_v = [pick(value_seg[g], RATE_FAR) for g in range(FAR_GROUPS)]
        far_s = [pick_ids(slide_seg[g], RATE_FAR) for g in range(FAR_GROUPS)]

        def per_group(index):
            query_blk = lax.dynamic_index_in_dim(query_seg, index, 0, False)
            key_blk = lax.dynamic_index_in_dim(key_seg, index, 0, False)
            value_blk = lax.dynamic_index_in_dim(value_seg, index, 0, False)
            slide_blk = lax.dynamic_index_in_dim(slide_seg, index, 0, False)
            local_max, local_tot, local_sum = lax.map(local_block, (query_blk.reshape(N_NARROW, TOK_DEV, D), key_blk.reshape(N_NARROW, TOK_DEV, D), value_blk.reshape(N_NARROW, TOK_DEV, D), slide_blk.reshape(N_NARROW, TOK_DEV)))
            parts = [(local_max.reshape(GROUP_TOK, HEADS), local_tot.reshape(GROUP_TOK, HEADS), local_sum.reshape(GROUP_TOK, HEADS, HDIM))]
            near_q = pick(query_blk, RATE_NEAR)
            near_qids = pick_ids(slide_blk, RATE_NEAR)
            base = (index // NEAR_GROUPS) * NEAR_GROUPS
            for member in range(NEAR_GROUPS):
                kidx = (base + member).astype(jnp.int32)
                parts.append(spread(attend(near_q, near_qids, lax.dynamic_index_in_dim(near_k, kidx, 0, False), lax.dynamic_index_in_dim(near_v, kidx, 0, False), lax.dynamic_index_in_dim(near_s, kidx, 0, False)), RATE_NEAR))
            far_q = pick(query_blk, RATE_FAR)
            far_qids = pick_ids(slide_blk, RATE_FAR)
            for member in range(FAR_GROUPS):
                parts.append(spread(attend(far_q, far_qids, far_k[member], far_v[member], far_s[member]), RATE_FAR))
            attended = combine(parts)
            return jnp.dot(attended, w_out, preferred_element_type=jnp.float32).astype(jnp.bfloat16)

        return lax.map(per_group, jnp.arange(FAR_GROUPS, dtype=jnp.int32)).reshape(SEG_FAR, D)

    encoded = lax.map(segment, (queries.reshape(segs, FAR_GROUPS, GROUP_TOK, D), keys.reshape(segs, FAR_GROUPS, GROUP_TOK, D), values.reshape(segs, FAR_GROUPS, GROUP_TOK, D), slide_ids.reshape(segs, FAR_GROUPS, GROUP_TOK)))
    return encoded.reshape(TOKENS, D)
```

```python
import jax
import jax.numpy as jnp
from jax import lax
from jax.experimental import pallas as pl
from jax.experimental.pallas import tpu as pltpu
from jax.sharding import PartitionSpec as P

MESH = pl.DeviceIdType.MESH
HEADS = 12
HDIM = 64
WIDTH = 768
TOK = 128
WIDE = 32
SEG = 8
REACH = 6
PARTNERS = 2 * REACH
PENALTY = 2048.0
ABSENT = -1e30
BF16 = jnp.bfloat16
F32 = jnp.float32

KV_PARTS = ((0, 5), (5, 4), (9, 4))


def lanes_of(shape):
    return lax.broadcasted_iota(jnp.int32, shape, len(shape) - 1)


def nt_dot(left, right):
    return lax.dot_general(left, right, (((1,), (1,)), ((), ())), preferred_element_type=F32)


def nn_dot(left, right):
    return lax.dot_general(left, right, (((1,), (0,)), ((), ())), preferred_element_type=F32)


def out_slot(sender_at, receiver_at):
    return lax.rem(sender_at - receiver_at + 15, 8) - (receiver_at < 7).astype(jnp.int32)


def kernel(
    q_ref, k_ref, v_ref, ids_ref, w_hbm, out_ref,
    pq, pk, pv, pc, kv_sel, q_sel, kv, kv_roll, q_in, q_out, q_roll, o_in, o_out, r_in, r_out,
    stat_in, stat_out, loc_o, loc_l, att, w_vmem,
    w_sem, pair_send, pair_recv, ring_send, ring_recv,
    q_send, q_recv_in, q_recv_out, o_send, o_recv_in, o_recv_out,
):
    g = lax.axis_index("wide")
    n = lax.axis_index("narrow")
    place = lax.rem(g, SEG)
    core = lax.rem(n, 2)
    pair = (g, n + 1 - 2 * core)
    right = (g, lax.rem(n + 2, 16))
    left = (g, lax.rem(n + 14, 16))

    def partner(i):
        offset = i - REACH + (i >= REACH).astype(jnp.int32)
        other = lax.rem(g + offset + WIDE, WIDE)
        return other, lax.rem(other, SEG), other // SEG == g // SEG

    empty = jnp.where(lax.rem(lanes_of((2, 16, 128)), 8) == 0, ABSENT, 0.0).astype(BF16)
    spare = SEG - 1 - place
    r_in[spare] = jnp.zeros((2, 7, 16, 128), BF16)
    r_in[spare, :, 0] = empty
    r_out[5] = jnp.zeros((2, 4, 16, 128), BF16)
    r_out[5, :, 0] = empty

    w_copy = pltpu.make_async_copy(w_hbm, w_vmem, w_sem)
    w_copy.start()

    barrier = pltpu.get_barrier_semaphore()
    for device in (pair, right, left):
        pl.semaphore_signal(barrier, inc=1, device_id=device, device_id_type=MESH)

    @pl.loop(0, PARTNERS)
    def _(i):
        other, _, _ = partner(i)
        for side in range(2):
            pl.semaphore_signal(
                barrier, inc=1, device_id=(other, n - core + side), device_id_type=MESH
            )

    row = lax.broadcasted_iota(jnp.int32, (TOK, TOK), 0)
    col = lax.broadcasted_iota(jnp.int32, (TOK, TOK), 1)
    order = (col == 8 * (row % 16) + row // 16).astype(F32).astype(BF16)
    unlike = (jnp.broadcast_to(ids_ref[...], (TOK, TOK)) != row % 16).astype(F32).astype(BF16)
    sorted_c = nt_dot(order, unlike)
    pc[...] = sorted_c.astype(BF16)
    lane16 = lanes_of((16, 128))
    low16 = lane16 < HDIM
    others = jnp.zeros((16, 128), F32)
    for residue in range(8):
        others = jnp.where(
            lane16 // 16 == residue, sorted_c[residue * 16:residue * 16 + 16], others
        )
    others = others.astype(BF16)
    for half in range(2):
        kv_sel[half, 0] = others
        q_sel[half, 0] = others

    def picked(source, a, shift):
        first = (2 * a + shift) % 8
        block = source[:, a * 128:(a + 1) * 128]
        return jnp.where(
            low16, block[first * 16:first * 16 + 16], block[first * 16 + 16:first * 16 + 32]
        ).astype(BF16)

    sorted_k = nn_dot(order, k_ref[...])
    pk[...] = sorted_k.astype(BF16)
    for a in range(6):
        for part in range(2):
            kv_sel[a // 3, 1 + 4 * (a % 3) + part] = picked(sorted_k, a, 4 * part)
    sorted_v = nn_dot(order, v_ref[...])
    pv[...] = sorted_v.astype(BF16)
    for a in range(6):
        for part in range(2):
            kv_sel[a // 3, 3 + 4 * (a % 3) + part] = picked(sorted_v, a, 4 * part)
    kv[core] = kv_sel[core]
    sorted_q = nn_dot(order, q_ref[...]) * (HDIM ** -0.5)
    pq[...] = sorted_q.astype(BF16)
    for a in range(6):
        for part in range(2):
            q_sel[a // 3, 1 + 3 * part + a % 3] = picked(sorted_q, a, 4 * part)
    q_in[place, core] = q_sel[core]

    pl.semaphore_wait(barrier, 3 + 2 * PARTNERS)

    pair_kv = pltpu.make_async_remote_copy(
        kv_sel.at[1 - core], kv.at[core], pair_send.at[0], pair_recv.at[0],
        device_id=pair, device_id_type=MESH,
    )
    pair_kv.start()
    pair_q = pltpu.make_async_remote_copy(
        q_sel.at[1 - core], q_in.at[place, core], pair_send.at[1], pair_recv.at[1],
        device_id=pair, device_id_type=MESH,
    )
    pair_q.start()

    def ring_copy(step, way, part):
        source = step if way == 0 else (8 - step) % 8
        target = source + 1 if way == 0 else (source + 7) % 8
        first, count = KV_PARTS[part]
        if step < 3:
            at, to, rows, arrived = 2 * source, 2 * target, 2, target
        else:
            at, to, rows, arrived = 2 * source + way, 2 * target + way, 1, 4 * (1 - way)
        return pltpu.make_async_remote_copy(
            kv.at[pl.ds(at, rows), pl.ds(first, count)],
            kv.at[pl.ds(to, rows), pl.ds(first, count)],
            ring_send.at[(step * 2 + way) * 3 + part],
            ring_recv.at[arrived * 3 + part],
            device_id=right if way == 0 else left, device_id_type=MESH,
        )

    def ring_step(step):
        for part in range(3):
            for way in range(2):
                if step > 0:
                    ring_copy(step - 1, way, part).wait_recv()
                if step < 4:
                    ring_copy(step, way, part).start()

    pair_kv.wait_recv()
    ring_step(0)

    def q_copy(i, side, inside):
        other, other_at, _ = partner(i)
        if inside:
            source, target, arrived = q_sel.at[side], q_in.at[place, core], q_recv_in.at[place, core]
        else:
            slot = out_slot(place, other_at)
            source, target = q_sel.at[side, pl.ds(0, 4)], q_out.at[slot, core]
            arrived = q_recv_out.at[slot, core]
        return pltpu.make_async_remote_copy(
            source, target, q_send.at[2 * i + side], arrived,
            device_id=(other, n - core + side), device_id_type=MESH,
        )

    def for_partners(act):
        @pl.loop(0, PARTNERS)
        def _(i):
            _, _, same = partner(i)

            @pl.when(same)
            def _():
                for side in range(2):
                    act(i, side, True)

            @pl.when(jnp.logical_not(same))
            def _():
                for side in range(2):
                    act(i, side, False)

    for_partners(lambda i, side, inside: q_copy(i, side, inside).start())

    ones = jnp.ones((TOK, 128), BF16)
    lane128 = lanes_of((TOK, 128))
    own_slide = jnp.where(lane128 < 16, (sorted_c - 1.0) * PENALTY, 0.0).astype(BF16)
    wide_low = lanes_of((TOK, 128)) < HDIM

    def local_pair(a):
        cols = slice(a * 128, (a + 1) * 128)
        block = pq[:, cols].astype(F32)
        left_side = jnp.concatenate(
            [
                jnp.concatenate([jnp.where(wide_low, block, 0.0).astype(BF16), own_slide], 1),
                jnp.concatenate([jnp.where(wide_low, 0.0, block).astype(BF16), own_slide], 1),
            ],
            0,
        )
        scores = nt_dot(left_side, jnp.concatenate([pk[:, cols], pc[...]], 1))
        top = jnp.max(scores, axis=1, keepdims=True)
        weights = jnp.exp(scores - top).astype(BF16)
        summed = nn_dot(weights, jnp.concatenate([pv[:, cols], ones], 1))
        result = summed[:, :128] / summed[:, 128:]
        level = top + jnp.log(summed[:, 128:])
        loc_o[:, cols] = jnp.where(wide_low, result[:TOK], result[TOK:])
        loc_l[:, cols] = jnp.where(wide_low, level[:TOK], level[TOK:])

    local_pair(0)
    local_pair(1)
    ring_step(1)
    local_pair(2)
    local_pair(3)
    ring_step(2)
    local_pair(4)
    local_pair(5)
    ring_step(3)

    pair_q.wait_recv()

    @pl.loop(0, PARTNERS)
    def _(i):
        other, other_at, same = partner(i)

        @pl.when(same)
        def _():
            for side in range(2):
                spot = q_in.at[other_at, side]
                pltpu.make_async_copy(spot, spot, q_recv_in.at[other_at, side]).wait()

        @pl.when(jnp.logical_not(same))
        def _():
            slot = out_slot(other_at, place)
            for side in range(2):
                spot = q_out.at[slot, side]
                pltpu.make_async_copy(spot, spot, q_recv_out.at[slot, side]).wait()

    for side in range(2):
        for slot in range(SEG):
            q_roll[slot, side] = pltpu.roll(q_in[slot, side, 0].astype(F32), 64, 1).astype(BF16)
    ring_step(4)
    for slot in range(16):
        kv_roll[slot] = pltpu.roll(kv[slot, 0].astype(F32), 64, 1).astype(BF16)

    stat_in[...] = jnp.zeros(stat_in.shape, F32)
    stat_out[...] = jnp.zeros(stat_out.shape, F32)
    many = jnp.ones((256, 128), BF16)
    half_masks = [
        jnp.where(low16, 1.0, 0.0).astype(BF16), jnp.where(low16, 0.0, 1.0).astype(BF16)
    ]

    def stacked(ref_value):
        return ref_value.reshape(-1, 128)

    def blocks(a, total, first, rows):
        low = lanes_of((rows, 128)) < HDIM
        return jnp.where(low, a[first:first + rows], a[total + first:total + first + rows])

    def group_pair(j):
        masks = []
        for u in range(2):
            residue = lax.rem(6 * core + 2 * j + u, 8)
            masks.append(jnp.where(lane16 // 16 == residue, PENALTY, 0.0).astype(BF16))
        near_c = stacked(kv[:, 0])
        turned_c = stacked(kv_roll[...])
        far_k = jnp.concatenate([stacked(kv[:, 1 + 4 * j]), near_c], 1)
        near_k = jnp.concatenate([stacked(kv[:, 2 + 4 * j]), turned_c], 1)
        far_v = jnp.concatenate([stacked(kv[:, 3 + 4 * j]), many], 1)
        near_v = jnp.concatenate([stacked(kv[:, 4 + 4 * j]), many], 1)

        def left_side(block, slides, u):
            return jnp.concatenate(
                [stacked(block * half_masks[u]), stacked((slides - 1) * masks[u])], 1
            )

        def levels(top, totals):
            return jnp.where(top < -PENALTY / 2, ABSENT, top + jnp.log(totals))

        def inside(first, count):
            rows = count * 32
            far_q, near_q = q_in[first:first + count, :, 1 + j], q_in[first:first + count, :, 4 + j]
            slides, turned = q_in[first:first + count, :, 0], q_roll[first:first + count]
            lhs = jnp.concatenate(
                [
                    left_side(far_q, slides, 0), left_side(near_q, turned, 0),
                    left_side(far_q, slides, 1), left_side(near_q, turned, 1),
                ],
                0,
            )
            far_s, near_s = nt_dot(lhs, far_k), nt_dot(lhs, near_k)
            top = jnp.max(jnp.maximum(far_s, near_s), axis=1, keepdims=True)
            far_o = nn_dot(jnp.exp(far_s - top).astype(BF16), far_v)
            near_o = nn_dot(jnp.exp(near_s - top).astype(BF16), near_v)
            both = far_o + near_o
            for part in range(2):
                at = [part * rows, (2 + part) * rows]
                outs, lev = [], []
                for start in at:
                    total = both[start:start + rows]
                    if part == 0:
                        total = total + far_o[start:start + rows]
                    outs.append(total[:, :128] / total[:, 128:])
                    lev.append(levels(top[start:start + rows], total[:, 128:]))
                low = lanes_of((rows, 128)) < HDIM
                o_in[first:first + count, :, 1 + 3 * part + j] = (
                    jnp.where(low, outs[0], outs[1]).astype(BF16).reshape(count, 2, 16, 128)
                )
                spot = lanes_of((rows, 128)) // 8
                kept = stacked(stat_in[first:first + count])
                for u in range(2):
                    kept = jnp.where(spot == 8 * part + 2 * j + u, lev[u], kept)
                stat_in[first:first + count] = kept.reshape(count, 2, 16, 128)

        def outside(first, count):
            rows = count * 32
            far_q, slides = q_out[first:first + count, :, 1 + j], q_out[first:first + count, :, 0]
            lhs = jnp.concatenate([left_side(far_q, slides, 0), left_side(far_q, slides, 1)], 0)
            far_s = nt_dot(lhs, far_k)
            top = jnp.max(far_s, axis=1, keepdims=True)
            total = nn_dot(jnp.exp(far_s - top).astype(BF16), far_v)
            result = total[:, :128] / total[:, 128:]
            lev = levels(top, total[:, 128:])
            low = lanes_of((rows, 128)) < HDIM
            o_out[first:first + count, :, 1 + j] = (
                jnp.where(low, result[:rows], result[rows:]).astype(BF16).reshape(count, 2, 16, 128)
            )
            spot = lanes_of((rows, 128)) // 8
            kept = stacked(stat_out[first:first + count])
            for u in range(2):
                kept = jnp.where(spot == 2 * j + u, lev[u * rows:(u + 1) * rows], kept)
            stat_out[first:first + count] = kept.reshape(count, 2, 16, 128)

        for first in range(0, 8, 2):
            inside(first, 2)
        for first in range(0, 6, 3):
            outside(first, 3)

    @pl.loop(0, 3)
    def _(j):
        group_pair(j)

    def in_pieces(level):
        high = level.astype(BF16).astype(F32)
        rest = level - high
        middle = rest.astype(BF16).astype(F32)
        last = rest - middle
        at = lax.rem(lanes_of(level.shape), 8)
        pieces = jnp.where(
            at == 0, high, jnp.where(at == 1, middle, jnp.where(at == 2, last, 0.0))
        )
        return pieces.astype(BF16)

    o_in[:, :, 0] = in_pieces(stat_in[...])
    o_out[:, :, 0] = in_pieces(stat_out[...])

    def o_copy(i, side, inside):
        other, other_at, _ = partner(i)
        if inside:
            source, target, arrived = o_in.at[other_at, side], r_in.at[place, core], o_recv_in.at[place, core]
        else:
            slot = out_slot(place, other_at)
            source, target = o_out.at[out_slot(other_at, place), side], r_out.at[slot, core]
            arrived = o_recv_out.at[slot, core]
        return pltpu.make_async_remote_copy(
            source, target, o_send.at[2 * i + side], arrived,
            device_id=(other, n - core + side), device_id_type=MESH,
        )

    for_partners(lambda i, side, inside: o_copy(i, side, inside).start())
    pair_o = pltpu.make_async_remote_copy(
        o_in.at[place, 1 - core], r_in.at[place, core], pair_send.at[2], pair_recv.at[2],
        device_id=pair, device_id_type=MESH,
    )
    pair_o.start()
    r_in[place, core] = o_in[place, core]
    att[...] = loc_o[...]

    @pl.loop(0, PARTNERS)
    def _(i):
        other, other_at, same = partner(i)

        @pl.when(same)
        def _():
            for side in range(2):
                spot = r_in.at[other_at, side]
                pltpu.make_async_copy(spot, spot, o_recv_in.at[other_at, side]).wait()

        @pl.when(jnp.logical_not(same))
        def _():
            slot = out_slot(other_at, place)
            for side in range(2):
                spot = r_out.at[slot, side]
                pltpu.make_async_copy(spot, spot, o_recv_out.at[slot, side]).wait()

    pair_o.wait_recv()

    e_row = lax.broadcasted_iota(jnp.int32, (128, 384), 0)
    e_col = lax.broadcasted_iota(jnp.int32, (128, 384), 1)
    to_far = jnp.where((e_row // 8 == e_col // 64) & (e_row % 8 < 3), 1.0, 0.0).astype(BF16)
    to_near = jnp.where((e_row // 8 == e_col // 64 + 8) & (e_row % 8 < 3), 1.0, 0.0).astype(BF16)
    for half in range(2):
        stats_i = r_in[:, half, 0].reshape(128, 128)
        stats_o = r_out[:, half, 0].reshape(96, 128)
        far_i = nn_dot(stats_i, to_far)
        near_i = nn_dot(stats_i, to_near)
        far_o = nn_dot(stats_o, to_far)
        for j in range(3):
            a = 3 * half + j
            lanes = slice(j * 128, (j + 1) * 128)
            cols = slice(a * 128, (a + 1) * 128)
            for part in range(2):
                r0 = (2 * a + 4 * part) % 8 * 16
                r1 = r0 + 16
                own_l = jnp.where(low16, loc_l[r0:r0 + 16, cols], loc_l[r1:r1 + 16, cols])
                own_o = jnp.where(low16, loc_o[r0:r0 + 16, cols], loc_o[r1:r1 + 16, cols])
                lev = (near_i if part else far_i)[:, lanes].reshape(8, 16, 128)
                val = r_in[:, half, 1 + 3 * part + j].astype(F32)
                if part == 0:
                    lev = jnp.concatenate([lev, far_o[:, lanes].reshape(6, 16, 128)], 0)
                    val = jnp.concatenate([val, r_out[:, half, 1 + j].astype(F32)], 0)
                top = jnp.maximum(jnp.max(lev, axis=0), own_l)
                scale = jnp.exp(lev - top[None])
                own_scale = jnp.exp(own_l - top)
                numer = jnp.sum(scale * val, axis=0) + own_scale * own_o
                denom = jnp.sum(scale, axis=0) + own_scale
                joined = numer / denom
                att[r0:r0 + 16, a * 128:a * 128 + 64] = joined[:, :64]
                att[r1:r1 + 16, a * 128 + 64:a * 128 + 128] = joined[:, 64:]

    back = (row == 8 * (col % 16) + col // 16).astype(F32).astype(BF16)
    attended = nn_dot(back, att[...].astype(BF16)).astype(BF16)
    w_copy.wait()
    out_ref[...] = nn_dot(attended, w_vmem[...]).astype(BF16)

    pair_kv.wait_send()
    pair_q.wait_send()
    pair_o.wait_send()
    for step in range(4):
        for way in range(2):
            for part in range(3):
                ring_copy(step, way, part).wait_send()

    def sent(i, side, inside):
        q_copy(i, side, inside).wait_send()
        o_copy(i, side, inside).wait_send()

    for_partners(sent)


def local(queries, keys, values, slide_ids, w_out):
    vmem = pl.BlockSpec(memory_space=pltpu.VMEM)
    dma = pltpu.SemaphoreType.DMA
    return pl.pallas_call(
        kernel,
        out_shape=jax.ShapeDtypeStruct((TOK, WIDTH), BF16),
        in_specs=[vmem, vmem, vmem, vmem, pl.BlockSpec(memory_space=pl.ANY)],
        out_specs=vmem,
        scratch_shapes=[
            pltpu.VMEM((TOK, WIDTH), BF16),
            pltpu.VMEM((TOK, WIDTH), BF16),
            pltpu.VMEM((TOK, WIDTH), BF16),
            pltpu.VMEM((TOK, 128), BF16),
            pltpu.VMEM((2, 13, 16, 128), BF16),
            pltpu.VMEM((2, 7, 16, 128), BF16),
            pltpu.VMEM((16, 13, 16, 128), BF16),
            pltpu.VMEM((16, 16, 128), BF16),
            pltpu.VMEM((8, 2, 7, 16, 128), BF16),
            pltpu.VMEM((6, 2, 4, 16, 128), BF16),
            pltpu.VMEM((8, 2, 16, 128), BF16),
            pltpu.VMEM((8, 2, 7, 16, 128), BF16),
            pltpu.VMEM((6, 2, 4, 16, 128), BF16),
            pltpu.VMEM((8, 2, 7, 16, 128), BF16),
            pltpu.VMEM((6, 2, 4, 16, 128), BF16),
            pltpu.VMEM((8, 2, 16, 128), F32),
            pltpu.VMEM((6, 2, 16, 128), F32),
            pltpu.VMEM((TOK, WIDTH), F32),
            pltpu.VMEM((TOK, WIDTH), F32),
            pltpu.VMEM((TOK, WIDTH), F32),
            pltpu.VMEM((WIDTH, WIDTH), BF16),
            dma,
            dma((3,)),
            dma((3,)),
            dma((24,)),
            dma((24,)),
            dma((24,)),
            dma((8, 2)),
            dma((6, 2)),
            dma((24,)),
            dma((8, 2)),
            dma((6, 2)),
        ],
        compiler_params=pltpu.CompilerParams(
            collective_id=0, has_side_effects=True, vmem_limit_bytes=40 * 1024 * 1024
        ),
        name="dilated",
    )(queries, keys, values, slide_ids.reshape(1, TOK), w_out)


def solution(mesh):
    placed = (
        P(("wide", "narrow"), None),
        P(("wide", "narrow"), None),
        P(("wide", "narrow"), None),
        P(("wide", "narrow")),
        P(),
    )
    return jax.shard_map(
        local, mesh=mesh, in_specs=placed, out_specs=P(("wide", "narrow"), None), check_vma=False
    )
```

```python
import jax
import jax.numpy as jnp
from jax import lax
from jax.experimental import pallas as pl
from jax.experimental.pallas import tpu as pltpu
from jax.sharding import PartitionSpec as P

MESH = pl.DeviceIdType.MESH
HEADS = 12
HDIM = 64
WIDTH = 768
TOK = 128
WIDE = 32
SEG = 8
REACH = 6
PARTNERS = 2 * REACH
PENALTY = 2048.0
ABSENT = -1e30
BF16 = jnp.bfloat16
F32 = jnp.float32

KV_PARTS = ((0, 5), (5, 4), (9, 4))


def lanes_of(shape):
    return lax.broadcasted_iota(jnp.int32, shape, len(shape) - 1)


def nt_dot(left, right):
    return lax.dot_general(left, right, (((1,), (1,)), ((), ())), preferred_element_type=F32)


def nn_dot(left, right):
    return lax.dot_general(left, right, (((1,), (0,)), ((), ())), preferred_element_type=F32)


def out_slot(sender_at, receiver_at):
    return lax.rem(sender_at - receiver_at + 15, 8) - (receiver_at < 7).astype(jnp.int32)


def kernel(
    q_hbm, k_hbm, v_hbm, ids_hbm, w_hbm, out_ref,
    q_ref, k_ref, v_ref, ids_ref,
    pq, pk, pv, pc, kv_sel, q_sel, kv, kv_roll, q_in, q_out, q_roll, o_in, o_out, r_in, r_out,
    loc_o, loc_l, att, w_vmem,
    in_sem, pair_send, pair_recv, ring_send, ring_recv,
    q_send, q_recv_in, q_recv_out, o_send_in, o_send_out, o_recv_in, o_recv_out,
):
    g = lax.axis_index("wide")
    n = lax.axis_index("narrow")
    place = lax.rem(g, SEG)
    core = lax.rem(n, 2)
    pair = (g, n + 1 - 2 * core)
    right = (g, lax.rem(n + 2, 16))
    left = (g, lax.rem(n + 14, 16))
    right2 = (g, lax.rem(n + 4, 16))
    left2 = (g, lax.rem(n + 12, 16))

    def partner(i):
        offset = i - REACH + (i >= REACH).astype(jnp.int32)
        other = lax.rem(g + offset + WIDE, WIDE)
        return other, lax.rem(other, SEG), other // SEG == g // SEG

    empty = jnp.where(lax.rem(lanes_of((2, 16, 128)), 8) == 0, ABSENT, 0.0).astype(BF16)
    spare = SEG - 1 - place
    r_in[spare] = jnp.zeros((2, 7, 16, 128), BF16)
    r_in[spare, :, 0] = empty
    r_out[5] = jnp.zeros((2, 4, 16, 128), BF16)
    r_out[5, :, 0] = empty

    loads = [
        pltpu.make_async_copy(source, target, in_sem.at[at])
        for at, (source, target) in enumerate(
            ((ids_hbm, ids_ref), (k_hbm, k_ref), (v_hbm, v_ref), (q_hbm, q_ref), (w_hbm, w_vmem))
        )
    ]
    for load in loads:
        load.start()

    barrier = pltpu.get_barrier_semaphore()
    turn = 1 - 2 * core
    crossed = ((g, right[1] + turn), (g, left[1] + turn))
    for device in (pair, right, left, right2, left2) + crossed:
        pl.semaphore_signal(barrier, inc=1, device_id=device, device_id_type=MESH)

    @pl.loop(0, PARTNERS)
    def _(i):
        other, _, _ = partner(i)
        for side in range(2):
            pl.semaphore_signal(
                barrier, inc=1, device_id=(other, n - core + side), device_id_type=MESH
            )

    row = lax.broadcasted_iota(jnp.int32, (TOK, TOK), 0)
    col = lax.broadcasted_iota(jnp.int32, (TOK, TOK), 1)
    order = (col == 8 * (row % 16) + row // 16).astype(F32).astype(BF16)
    loads[0].wait()
    unlike = (jnp.broadcast_to(ids_ref[...], (TOK, TOK)) != row % 16).astype(F32).astype(BF16)
    sorted_c = nt_dot(order, unlike)
    pc[...] = sorted_c.astype(BF16)
    lane16 = lanes_of((16, 128))
    low16 = lane16 < HDIM
    others = jnp.zeros((16, 128), F32)
    for residue in range(8):
        others = jnp.where(
            lane16 // 16 == residue, sorted_c[residue * 16:residue * 16 + 16], others
        )
    others = others.astype(BF16)
    for half in range(2):
        kv_sel[half, 0] = others
        q_sel[half, 0] = others

    def picked(source, a, shift):
        first = (2 * a + shift) % 8
        block = source[:, a * 128:(a + 1) * 128]
        return jnp.where(
            low16, block[first * 16:first * 16 + 16], block[first * 16 + 16:first * 16 + 32]
        ).astype(BF16)

    loads[1].wait()
    sorted_k = nn_dot(order, k_ref[...])
    pk[...] = sorted_k.astype(BF16)
    for a in range(6):
        for part in range(2):
            kv_sel[a // 3, 1 + 4 * (a % 3) + part] = picked(sorted_k, a, 4 * part)
    loads[2].wait()
    sorted_v = nn_dot(order, v_ref[...])
    pv[...] = sorted_v.astype(BF16)
    for a in range(6):
        for part in range(2):
            kv_sel[a // 3, 3 + 4 * (a % 3) + part] = picked(sorted_v, a, 4 * part)
    kv[core] = kv_sel[core]
    loads[3].wait()
    sorted_q = nn_dot(order, q_ref[...]) * (HDIM ** -0.5)
    pq[...] = sorted_q.astype(BF16)
    for a in range(6):
        for part in range(2):
            q_sel[a // 3, 1 + 3 * part + a % 3] = picked(sorted_q, a, 4 * part)
    q_in[place, core] = q_sel[core]

    pl.semaphore_wait(barrier, 7 + 2 * PARTNERS)

    def send(source, target, sent, arrived, device):
        return pltpu.make_async_remote_copy(
            source, target, ring_send.at[sent], ring_recv.at[arrived],
            device_id=device, device_id_type=MESH,
        )

    def pair_kv(part):
        first, count = KV_PARTS[part]
        rows = pl.ds(first, count)
        return send(
            kv_sel.at[1 - core, rows], kv.at[core, rows], part, core * 3 + part, pair
        )

    def pair_kv_arrival(part):
        first, count = KV_PARTS[part]
        rows = pl.ds(first, count)
        other = 1 - core
        return send(kv_sel.at[core, rows], kv.at[other, rows], part, other * 3 + part, pair)

    def first_kv(way, part, side):
        first, count = KV_PARTS[part]
        rows = pl.ds(first, count)
        slot = (2, 14)[way] + core
        device = (g, lax.rem(n - core + (2, 14)[way], 16) + side)
        return send(
            kv_sel.at[side, rows], kv.at[slot, rows],
            3 + (way * 3 + part) * 2 + side, slot * 3 + part, device,
        )

    def first_arrival(way, part, side):
        first, count = KV_PARTS[part]
        rows = pl.ds(first, count)
        slot = (2, 14)[way] + side
        return send(
            kv_sel.at[0, rows], kv.at[slot, rows],
            3 + (way * 3 + part) * 2 + side, slot * 3 + part, pair,
        )

    def passed(kind, way, part):
        first, count = KV_PARTS[part]
        rows = pl.ds(first, count)
        at, to = (((2, 4), (4, 6), (4, 8)), ((14, 12), (12, 10), (13, 9)))[way][kind]
        slots = 1 if kind == 2 else 2
        device = ((right, right, right2), (left, left, left2))[way][kind]
        return send(
            kv.at[pl.ds(at, slots), rows], kv.at[pl.ds(to, slots), rows],
            15 + (kind * 2 + way) * 3 + part, to * 3 + part, device,
        )

    both_ways = [(part, way) for part in range(3) for way in range(2)]
    for part, way in both_ways:
        for side in range(2):
            first_kv(way, part, side).start()
        if way == 1:
            pair_kv(part).start()
    pair_q = pltpu.make_async_remote_copy(
        q_sel.at[1 - core], q_in.at[place, core], pair_send.at[0], pair_recv.at[0],
        device_id=pair, device_id_type=MESH,
    )
    pair_q.start()

    def pass_on(stage):
        for part, way in both_ways:
            if stage == 0:
                for side in range(2):
                    first_arrival(way, part, side).wait_recv()
                passed(0, way, part).start()
            else:
                passed(0, way, part).wait_recv()
                passed(1, way, part).start()
                passed(2, way, part).start()

    def q_copy(i, side, inside):
        other, other_at, _ = partner(i)
        if inside:
            source, target, arrived = q_sel.at[side], q_in.at[place, core], q_recv_in.at[place, core]
        else:
            slot = out_slot(place, other_at)
            source, target = q_sel.at[side, pl.ds(0, 4)], q_out.at[slot, core]
            arrived = q_recv_out.at[slot, core]
        return pltpu.make_async_remote_copy(
            source, target, q_send.at[2 * i + side], arrived,
            device_id=(other, n - core + side), device_id_type=MESH,
        )

    def for_partners(act):
        @pl.loop(0, PARTNERS)
        def _(i):
            _, _, same = partner(i)

            @pl.when(same)
            def _():
                for side in range(2):
                    act(i, side, True)

            @pl.when(jnp.logical_not(same))
            def _():
                for side in range(2):
                    act(i, side, False)

    for_partners(lambda i, side, inside: q_copy(i, side, inside).start())

    ones = jnp.ones((TOK, 128), BF16)
    lane128 = lanes_of((TOK, 128))
    own_slide = jnp.where(lane128 < 16, (sorted_c - 1.0) * PENALTY, 0.0).astype(BF16)
    wide_low = lanes_of((TOK, 128)) < HDIM

    def local_pair(a):
        cols = slice(a * 128, (a + 1) * 128)
        block = pq[:, cols].astype(F32)
        left_side = jnp.concatenate(
            [
                jnp.concatenate([jnp.where(wide_low, block, 0.0).astype(BF16), own_slide], 1),
                jnp.concatenate([jnp.where(wide_low, 0.0, block).astype(BF16), own_slide], 1),
            ],
            0,
        )
        scores = nt_dot(left_side, jnp.concatenate([pk[:, cols], pc[...]], 1))
        top = jnp.max(scores, axis=1, keepdims=True)
        weights = jnp.exp(scores - top).astype(BF16)
        summed = nn_dot(weights, jnp.concatenate([pv[:, cols], ones], 1))
        result = summed[:, :128] / summed[:, 128:]
        level = top + jnp.log(summed[:, 128:])
        loc_o[:, cols] = jnp.where(wide_low, result[:TOK], result[TOK:])
        loc_l[:, cols] = jnp.where(wide_low, level[:TOK], level[TOK:])

    local_pair(0)
    local_pair(1)
    pass_on(0)
    local_pair(2)
    local_pair(3)
    pass_on(1)
    local_pair(4)
    local_pair(5)

    pair_q.wait_recv()

    @pl.loop(0, PARTNERS)
    def _(i):
        other, other_at, same = partner(i)

        @pl.when(same)
        def _():
            for side in range(2):
                spot = q_in.at[other_at, side]
                pltpu.make_async_copy(spot, spot, q_recv_in.at[other_at, side]).wait()

        @pl.when(jnp.logical_not(same))
        def _():
            slot = out_slot(other_at, place)
            for side in range(2):
                spot = q_out.at[slot, side]
                pltpu.make_async_copy(spot, spot, q_recv_out.at[slot, side]).wait()

    for side in range(2):
        for slot in range(SEG):
            q_roll[slot, side] = pltpu.roll(q_in[slot, side, 0].astype(F32), 64, 1).astype(BF16)
    for part in range(3):
        pair_kv_arrival(part).wait_recv()
        for way in range(2):
            passed(1, way, part).wait_recv()
            passed(2, way, part).wait_recv()
    for slot in range(16):
        kv_roll[slot] = pltpu.roll(kv[slot, 0].astype(F32), 64, 1).astype(BF16)

    many = jnp.ones((256, 128), BF16)
    half_masks = [
        jnp.where(low16, 1.0, 0.0).astype(BF16), jnp.where(low16, 0.0, 1.0).astype(BF16)
    ]
    masks = []
    for head in range(6):
        residue = lax.rem(6 * core + head, 8)
        masks.append(jnp.where(lane16 // 16 == residue, PENALTY, 0.0).astype(BF16))

    def stacked(value):
        return value.reshape(-1, 128)

    def left_side(block, slides, head):
        return jnp.concatenate(
            [stacked(block * half_masks[head % 2]), stacked((slides - 1) * masks[head])], 1
        )

    def levels(top, totals):
        return jnp.where(top < -PENALTY / 2, ABSENT, top + jnp.log(totals))

    def in_pieces(level):
        high = level.astype(BF16).astype(F32)
        rest = level - high
        middle = rest.astype(BF16).astype(F32)
        last = rest - middle
        at = lax.rem(lanes_of(level.shape), 8)
        pieces = jnp.where(
            at == 0, high, jnp.where(at == 1, middle, jnp.where(at == 2, last, 0.0))
        )
        return pieces.astype(BF16)

    def keys_of(part, j):
        slides = kv_roll[...] if part else kv[:, 0]
        return jnp.concatenate([stacked(kv[:, 1 + part + 4 * j]), stacked(slides)], 1)

    def values_of(part, j):
        return jnp.concatenate([stacked(kv[:, 3 + part + 4 * j]), many], 1)

    def inside(first, count):
        rows = count * 32
        span = pl.ds(first, count)
        low = lanes_of((rows, 128)) < HDIM
        spot = lanes_of((rows, 128)) // 8
        stats = jnp.zeros((rows, 128), F32)
        slides, turned = q_in[span, :, 0], q_roll[span]
        for j in range(3):
            far_q, near_q = q_in[span, :, 1 + j], q_in[span, :, 4 + j]
            lhs = jnp.concatenate(
                [
                    left_side(far_q, slides, 2 * j), left_side(near_q, turned, 2 * j),
                    left_side(far_q, slides, 2 * j + 1), left_side(near_q, turned, 2 * j + 1),
                ],
                0,
            )
            far_s, near_s = nt_dot(lhs, keys_of(0, j)), nt_dot(lhs, keys_of(1, j))
            top = jnp.max(jnp.maximum(far_s, near_s), axis=1, keepdims=True)
            far_o = nn_dot(jnp.exp(far_s - top).astype(BF16), values_of(0, j))
            both = far_o + nn_dot(jnp.exp(near_s - top).astype(BF16), values_of(1, j))
            for part in range(2):
                outs = []
                for u in range(2):
                    start = (2 * u + part) * rows
                    total = both[start:start + rows]
                    if part == 0:
                        total = total + far_o[start:start + rows]
                    outs.append(total[:, :128] / total[:, 128:])
                    level = levels(top[start:start + rows], total[:, 128:])
                    stats = jnp.where(spot == 8 * part + 2 * j + u, level, stats)
                o_in[span, :, 1 + 3 * part + j] = (
                    jnp.where(low, outs[0], outs[1]).astype(BF16).reshape(count, 2, 16, 128)
                )
        o_in[span, :, 0] = in_pieces(stats).reshape(count, 2, 16, 128)

    def outside(first, count):
        rows = count * 32
        span = pl.ds(first, count)
        low = lanes_of((rows, 128)) < HDIM
        spot = lanes_of((rows, 128)) // 8
        stats = jnp.zeros((rows, 128), F32)
        slides = q_out[span, :, 0]
        for j in range(3):
            far_q = q_out[span, :, 1 + j]
            lhs = jnp.concatenate(
                [left_side(far_q, slides, 2 * j), left_side(far_q, slides, 2 * j + 1)], 0
            )
            far_s = nt_dot(lhs, keys_of(0, j))
            top = jnp.max(far_s, axis=1, keepdims=True)
            total = nn_dot(jnp.exp(far_s - top).astype(BF16), values_of(0, j))
            result = total[:, :128] / total[:, 128:]
            level = levels(top, total[:, 128:])
            for u in range(2):
                stats = jnp.where(spot == 2 * j + u, level[u * rows:(u + 1) * rows], stats)
            o_out[span, :, 1 + j] = (
                jnp.where(low, result[:rows], result[rows:]).astype(BF16).reshape(count, 2, 16, 128)
            )
        o_out[span, :, 0] = in_pieces(stats).reshape(count, 2, 16, 128)

    def back_in(at, side):
        return pltpu.make_async_remote_copy(
            o_in.at[at, side], r_in.at[place, core], o_send_in.at[at, side],
            o_recv_in.at[place, core],
            device_id=(g - place + at, n - core + side), device_id_type=MESH,
        )

    def back_out(slot, side):
        at = lax.rem(slot + (place < 7).astype(jnp.int32) + place + 1, SEG)
        away = jnp.where(at > place, -SEG, SEG)
        other = lax.rem(g - place + at + away + WIDE, WIDE)
        return pltpu.make_async_remote_copy(
            o_out.at[slot, side], r_out.at[out_slot(place, at), core], o_send_out.at[slot, side],
            o_recv_out.at[out_slot(place, at), core],
            device_id=(other, n - core + side), device_id_type=MESH,
        )

    def if_near(at, act):
        apart = jnp.abs(at - place)

        @pl.when(jnp.logical_and(apart > 0, apart <= REACH))
        def _():
            for side in range(2):
                act(at, side)

    def if_used(slot, act):
        @pl.when(jnp.logical_or(slot < 5, lax.rem(place, 7) == 0))
        def _():
            for side in range(2):
                act(slot, side)

    @pl.loop(0, 2)
    def _(chunk):
        outside(3 * chunk, 3)
        for k in range(3):
            if_used(3 * chunk + k, lambda slot, side: back_out(slot, side).start())

    @pl.loop(0, 4)
    def _(chunk):
        inside(2 * chunk, 2)
        for k in range(2):
            if_near(2 * chunk + k, lambda at, side: back_in(at, side).start())

    pair_o = pltpu.make_async_remote_copy(
        o_in.at[place, 1 - core], r_in.at[place, core], pair_send.at[1], pair_recv.at[1],
        device_id=pair, device_id_type=MESH,
    )
    pair_o.start()
    r_in[place, core] = o_in[place, core]
    att[...] = loc_o[...]

    @pl.loop(0, PARTNERS)
    def _(i):
        other, other_at, same = partner(i)

        @pl.when(same)
        def _():
            for side in range(2):
                spot = r_in.at[other_at, side]
                pltpu.make_async_copy(spot, spot, o_recv_in.at[other_at, side]).wait()

        @pl.when(jnp.logical_not(same))
        def _():
            slot = out_slot(other_at, place)
            for side in range(2):
                spot = r_out.at[slot, side]
                pltpu.make_async_copy(spot, spot, o_recv_out.at[slot, side]).wait()

    pair_o.wait_recv()

    e_row = lax.broadcasted_iota(jnp.int32, (128, 384), 0)
    e_col = lax.broadcasted_iota(jnp.int32, (128, 384), 1)
    to_far = jnp.where((e_row // 8 == e_col // 64) & (e_row % 8 < 3), 1.0, 0.0).astype(BF16)
    to_near = jnp.where((e_row // 8 == e_col // 64 + 8) & (e_row % 8 < 3), 1.0, 0.0).astype(BF16)
    for half in range(2):
        stats_i = r_in[:, half, 0].reshape(128, 128)
        stats_o = r_out[:, half, 0].reshape(96, 128)
        far_i = nn_dot(stats_i, to_far)
        near_i = nn_dot(stats_i, to_near)
        far_o = nn_dot(stats_o, to_far)
        for j in range(3):
            a = 3 * half + j
            lanes = slice(j * 128, (j + 1) * 128)
            cols = slice(a * 128, (a + 1) * 128)
            for part in range(2):
                r0 = (2 * a + 4 * part) % 8 * 16
                r1 = r0 + 16
                own_l = jnp.where(low16, loc_l[r0:r0 + 16, cols], loc_l[r1:r1 + 16, cols])
                own_o = jnp.where(low16, loc_o[r0:r0 + 16, cols], loc_o[r1:r1 + 16, cols])
                lev = (near_i if part else far_i)[:, lanes].reshape(8, 16, 128)
                val = r_in[:, half, 1 + 3 * part + j].astype(F32)
                if part == 0:
                    lev = jnp.concatenate([lev, far_o[:, lanes].reshape(6, 16, 128)], 0)
                    val = jnp.concatenate([val, r_out[:, half, 1 + j].astype(F32)], 0)
                top = jnp.maximum(jnp.max(lev, axis=0), own_l)
                scale = jnp.exp(lev - top[None])
                own_scale = jnp.exp(own_l - top)
                numer = jnp.sum(scale * val, axis=0) + own_scale * own_o
                denom = jnp.sum(scale, axis=0) + own_scale
                joined = numer / denom
                att[r0:r0 + 16, a * 128:a * 128 + 64] = joined[:, :64]
                att[r1:r1 + 16, a * 128 + 64:a * 128 + 128] = joined[:, 64:]

    back = (row == 8 * (col % 16) + col // 16).astype(F32).astype(BF16)
    attended = nn_dot(back, att[...].astype(BF16)).astype(BF16)
    loads[4].wait()
    out_ref[...] = nn_dot(attended, w_vmem[...]).astype(BF16)

    pair_q.wait_send()
    pair_o.wait_send()
    for part, way in both_ways:
        for side in range(2):
            first_kv(way, part, side).wait_send()
        if way == 1:
            pair_kv(part).wait_send()
        for kind in range(3):
            passed(kind, way, part).wait_send()
    for_partners(lambda i, side, inside: q_copy(i, side, inside).wait_send())

    @pl.loop(0, 6)
    def _(slot):
        if_used(slot, lambda slot, side: back_out(slot, side).wait_send())

    @pl.loop(0, SEG)
    def _(at):
        if_near(at, lambda at, side: back_in(at, side).wait_send())


def local(queries, keys, values, slide_ids, w_out):
    vmem = pl.BlockSpec(memory_space=pltpu.VMEM)
    dma = pltpu.SemaphoreType.DMA
    return pl.pallas_call(
        kernel,
        out_shape=jax.ShapeDtypeStruct((TOK, WIDTH), BF16),
        in_specs=[pl.BlockSpec(memory_space=pltpu.HBM)] * 5,
        out_specs=vmem,
        scratch_shapes=[
            pltpu.VMEM((TOK, WIDTH), BF16),
            pltpu.VMEM((TOK, WIDTH), BF16),
            pltpu.VMEM((TOK, WIDTH), BF16),
            pltpu.VMEM((1, TOK), jnp.int32),
            pltpu.VMEM((TOK, WIDTH), BF16),
            pltpu.VMEM((TOK, WIDTH), BF16),
            pltpu.VMEM((TOK, WIDTH), BF16),
            pltpu.VMEM((TOK, 128), BF16),
            pltpu.VMEM((2, 13, 16, 128), BF16),
            pltpu.VMEM((2, 7, 16, 128), BF16),
            pltpu.VMEM((16, 13, 16, 128), BF16),
            pltpu.VMEM((16, 16, 128), BF16),
            pltpu.VMEM((8, 2, 7, 16, 128), BF16),
            pltpu.VMEM((6, 2, 4, 16, 128), BF16),
            pltpu.VMEM((8, 2, 16, 128), BF16),
            pltpu.VMEM((8, 2, 7, 16, 128), BF16),
            pltpu.VMEM((6, 2, 4, 16, 128), BF16),
            pltpu.VMEM((8, 2, 7, 16, 128), BF16),
            pltpu.VMEM((6, 2, 4, 16, 128), BF16),
            pltpu.VMEM((TOK, WIDTH), F32),
            pltpu.VMEM((TOK, WIDTH), F32),
            pltpu.VMEM((TOK, WIDTH), F32),
            pltpu.VMEM((WIDTH, WIDTH), BF16),
            dma((5,)),
            dma((2,)),
            dma((2,)),
            dma((33,)),
            dma((48,)),
            dma((24,)),
            dma((8, 2)),
            dma((6, 2)),
            dma((8, 2)),
            dma((6, 2)),
            dma((8, 2)),
            dma((6, 2)),
        ],
        compiler_params=pltpu.CompilerParams(
            collective_id=0, has_side_effects=True, vmem_limit_bytes=(63 * 1024 + 512) * 1024
        ),
        name="dilated",
    )(queries, keys, values, slide_ids.reshape(1, TOK), w_out)


def solution(mesh):
    placed = (
        P(("wide", "narrow"), None),
        P(("wide", "narrow"), None),
        P(("wide", "narrow"), None),
        P(("wide", "narrow")),
        P(),
    )
    return jax.shard_map(
        local, mesh=mesh, in_specs=placed, out_specs=P(("wide", "narrow"), None), check_vma=False
    )
```

```python
import jax
import jax.numpy as jnp
from jax import lax
from jax.experimental import pallas as pl
from jax.experimental.pallas import tpu as pltpu
from jax.sharding import PartitionSpec as P

MESH = pl.DeviceIdType.MESH
HEADS = 12
HDIM = 64
WIDTH = 768
TOK = 128
WIDE = 32
SEG = 8
REACH = 6
PARTNERS = 2 * REACH
PENALTY = 2048.0
ABSENT = -1e30
BF16 = jnp.bfloat16
F32 = jnp.float32

KV_PARTS = ((0, 4), (4, 3), (7, 3), (10, 3))
PARTS = len(KV_PARTS)
SLOTS = 2


def lanes_of(shape):
    return lax.broadcasted_iota(jnp.int32, shape, len(shape) - 1)


def nt_dot(left, right):
    return lax.dot_general(left, right, (((1,), (1,)), ((), ())), preferred_element_type=F32)


def nn_dot(left, right):
    return lax.dot_general(left, right, (((1,), (0,)), ((), ())), preferred_element_type=F32)


def out_slot(sender_at, receiver_at):
    return lax.rem(sender_at - receiver_at + 15, 8) - (receiver_at < 7).astype(jnp.int32)


def kernel(
    q_hbm, k_hbm, v_hbm, ids_hbm, w_hbm, out_ref,
    q_ref, k_ref, v_ref, ids_ref,
    pq, pk, pv, pc, kv_sel, q_sel, kv, kv_roll, q_in, q_out, q_roll, o_in, o_out, r_in, r_out,
    loc_o, loc_l, att, w_vmem,
    in_sem, pair_send, pair_recv, ring_send, ring_recv,
    q_send, q_recv_in, q_recv_out, o_send_in, o_send_out, o_recv_in, o_recv_out,
):
    g = lax.axis_index("wide")
    n = lax.axis_index("narrow")
    place = lax.rem(g, SEG)
    core = lax.rem(n, 2)
    pair = (g, n + 1 - 2 * core)
    right = (g, lax.rem(n + 2, 16))
    left = (g, lax.rem(n + 14, 16))
    right2 = (g, lax.rem(n + 4, 16))
    left2 = (g, lax.rem(n + 12, 16))

    def partner(i):
        offset = i - REACH + (i >= REACH).astype(jnp.int32)
        other = lax.rem(g + offset + WIDE, WIDE)
        return other, lax.rem(other, SEG), other // SEG == g // SEG

    empty = jnp.where(lax.rem(lanes_of((2, 16, 128)), 8) == 0, ABSENT, 0.0).astype(BF16)
    spare = SEG - 1 - place
    r_in[spare] = jnp.zeros((2, 7, 16, 128), BF16)
    r_in[spare, :, 0] = empty
    r_out[5] = jnp.zeros((2, 4, 16, 128), BF16)
    r_out[5, :, 0] = empty

    loads = [
        pltpu.make_async_copy(source, target, in_sem.at[at])
        for at, (source, target) in enumerate(
            ((ids_hbm, ids_ref), (k_hbm, k_ref), (v_hbm, v_ref), (q_hbm, q_ref), (w_hbm, w_vmem))
        )
    ]
    for load in loads[:4]:
        load.start()

    barrier = pltpu.get_barrier_semaphore()
    turn = 1 - 2 * core
    crossed = ((g, right[1] + turn), (g, left[1] + turn))
    for device in (pair, right, left, right2, left2) + crossed:
        pl.semaphore_signal(barrier, inc=1, device_id=device, device_id_type=MESH)

    for apart in range(-REACH, REACH + 1):
        if apart:
            for side in range(2):
                pl.semaphore_signal(
                    barrier, inc=1, device_id_type=MESH,
                    device_id=(lax.rem(g + apart + WIDE, WIDE), n - core + side),
                )

    row = lax.broadcasted_iota(jnp.int32, (TOK, TOK), 0)
    col = lax.broadcasted_iota(jnp.int32, (TOK, TOK), 1)
    order = (col == 8 * (row % 16) + row // 16).astype(F32).astype(BF16)
    loads[0].wait()
    unlike = (jnp.broadcast_to(ids_ref[...], (TOK, TOK)) != row % 16).astype(F32).astype(BF16)
    sorted_c = nt_dot(order, unlike)
    pc[...] = sorted_c.astype(BF16)
    lane16 = lanes_of((16, 128))
    low16 = lane16 < HDIM
    others = jnp.zeros((16, 128), F32)
    for residue in range(8):
        others = jnp.where(
            lane16 // 16 == residue, sorted_c[residue * 16:residue * 16 + 16], others
        )
    others = others.astype(BF16)
    for half in range(2):
        kv_sel[half, 0] = others
        q_sel[half, 0] = others

    def picked(source, a, shift):
        first = (2 * a + shift) % 8
        block = source[:, a * 128:(a + 1) * 128]
        return jnp.where(
            low16, block[first * 16:first * 16 + 16], block[first * 16 + 16:first * 16 + 32]
        ).astype(BF16)

    loads[1].wait()
    sorted_k = nn_dot(order, k_ref[...])
    pk[...] = sorted_k.astype(BF16)
    for a in range(6):
        for part in range(2):
            kv_sel[a // 3, 1 + 2 * (a % 3) + 6 * part] = picked(sorted_k, a, 4 * part)
    loads[2].wait()
    sorted_v = nn_dot(order, v_ref[...])
    pv[...] = sorted_v.astype(BF16)
    for a in range(6):
        for part in range(2):
            kv_sel[a // 3, 2 + 2 * (a % 3) + 6 * part] = picked(sorted_v, a, 4 * part)
    kv[core] = kv_sel[core]
    pl.semaphore_wait(barrier, 7 + 2 * PARTNERS)

    def send(source, target, sent, arrived, device):
        return pltpu.make_async_remote_copy(
            source, target, ring_send.at[sent], ring_recv.at[arrived],
            device_id=device, device_id_type=MESH,
        )

    def pair_kv(part):
        first, count = KV_PARTS[part]
        rows = pl.ds(first, count)
        return send(
            kv_sel.at[1 - core, rows], kv.at[core, rows], part, core * PARTS + part, pair
        )

    def pair_kv_arrival(part):
        first, count = KV_PARTS[part]
        rows = pl.ds(first, count)
        other = 1 - core
        return send(kv_sel.at[core, rows], kv.at[other, rows], part, other * PARTS + part, pair)

    def first_kv(way, part, side):
        first, count = KV_PARTS[part]
        rows = pl.ds(first, count)
        slot = (2, 14)[way] + core
        device = (g, lax.rem(n - core + (2, 14)[way], 16) + side)
        return send(
            kv_sel.at[side, rows], kv.at[slot, rows],
            PARTS + (way * PARTS + part) * 2 + side, slot * PARTS + part, device,
        )

    def first_arrival(way, part, side):
        first, count = KV_PARTS[part]
        rows = pl.ds(first, count)
        slot = (2, 14)[way] + side
        return send(
            kv_sel.at[0, rows], kv.at[slot, rows],
            PARTS + (way * PARTS + part) * 2 + side, slot * PARTS + part, pair,
        )

    def passed(kind, way, part):
        first, count = KV_PARTS[part]
        rows = pl.ds(first, count)
        at, to = (((2, 4), (4, 6), (4, 8)), ((14, 12), (12, 10), (13, 9)))[way][kind]
        slots = 1 if kind == 2 else 2
        device = ((right, right, right2), (left, left, left2))[way][kind]
        return send(
            kv.at[pl.ds(at, slots), rows], kv.at[pl.ds(to, slots), rows],
            5 * PARTS + (kind * 2 + way) * PARTS + part, to * PARTS + part, device,
        )

    both_ways = [(part, way) for part in range(PARTS) for way in range(2)]
    for part, way in both_ways:
        for side in range(2):
            first_kv(way, part, side).start()
        if way == 1:
            pair_kv(part).start()
    loads[3].wait()
    sorted_q = nn_dot(order, q_ref[...]) * (HDIM ** -0.5)
    pq[...] = sorted_q.astype(BF16)
    for a in range(6):
        for part in range(2):
            q_sel[a // 3, 1 + 3 * part + a % 3] = picked(sorted_q, a, 4 * part)
    q_in[place, core] = q_sel[core]
    loads[4].start()

    pair_q = pltpu.make_async_remote_copy(
        q_sel.at[1 - core], q_in.at[place, core], pair_send.at[0], pair_recv.at[0],
        device_id=pair, device_id_type=MESH,
    )
    pair_q.start()

    def pass_on(stage):
        for part, way in both_ways:
            if stage == 0:
                for side in range(2):
                    first_arrival(way, part, side).wait_recv()
                passed(0, way, part).start()
            else:
                passed(0, way, part).wait_recv()
                passed(1, way, part).start()
                passed(2, way, part).start()

    def q_copy(i, side, inside):
        other, other_at, _ = partner(i)
        if inside:
            source, target, arrived = q_sel.at[side], q_in.at[place, core], q_recv_in.at[place, core]
        else:
            slot = out_slot(place, other_at)
            source, target = q_sel.at[side, pl.ds(0, 4)], q_out.at[slot, core]
            arrived = q_recv_out.at[slot, core]
        return pltpu.make_async_remote_copy(
            source, target, q_send.at[2 * i + side], arrived,
            device_id=(other, n - core + side), device_id_type=MESH,
        )

    def for_partners(act):
        @pl.loop(0, PARTNERS)
        def _(i):
            _, _, same = partner(i)

            @pl.when(same)
            def _():
                for side in range(2):
                    act(i, side, True)

            @pl.when(jnp.logical_not(same))
            def _():
                for side in range(2):
                    act(i, side, False)

    for_partners(lambda i, side, inside: q_copy(i, side, inside).start())

    ones = jnp.ones((TOK, 128), BF16)
    lane128 = lanes_of((TOK, 128))
    own_slide = jnp.where(lane128 < 16, (sorted_c - 1.0) * PENALTY, 0.0).astype(BF16)
    wide_low = lanes_of((TOK, 128)) < HDIM

    def local_pair(a):
        cols = slice(a * 128, (a + 1) * 128)
        block = pq[:, cols].astype(F32)
        left_side = jnp.concatenate(
            [
                jnp.concatenate([jnp.where(wide_low, block, 0.0).astype(BF16), own_slide], 1),
                jnp.concatenate([jnp.where(wide_low, 0.0, block).astype(BF16), own_slide], 1),
            ],
            0,
        )
        scores = nt_dot(left_side, jnp.concatenate([pk[:, cols], pc[...]], 1))
        top = jnp.max(scores, axis=1, keepdims=True)
        weights = jnp.exp(scores - top).astype(BF16)
        summed = nn_dot(weights, jnp.concatenate([pv[:, cols], ones], 1))
        result = summed[:, :128] / summed[:, 128:]
        level = top + jnp.log(summed[:, 128:])
        loc_o[:, cols] = jnp.where(wide_low, result[:TOK], result[TOK:])
        loc_l[:, cols] = jnp.where(wide_low, level[:TOK], level[TOK:])

    local_pair(0)
    local_pair(1)
    pass_on(0)
    local_pair(2)
    local_pair(3)
    pass_on(1)
    local_pair(4)
    local_pair(5)

    pair_q.wait_recv()

    @pl.loop(0, PARTNERS)
    def _(i):
        other, other_at, same = partner(i)

        @pl.when(same)
        def _():
            for side in range(2):
                spot = q_in.at[other_at, side]
                pltpu.make_async_copy(spot, spot, q_recv_in.at[other_at, side]).wait()

        @pl.when(jnp.logical_not(same))
        def _():
            slot = out_slot(other_at, place)
            for side in range(2):
                spot = q_out.at[slot, side]
                pltpu.make_async_copy(spot, spot, q_recv_out.at[slot, side]).wait()

    for side in range(2):
        for slot in range(SEG):
            q_roll[slot, side] = pltpu.roll(q_in[slot, side, 0].astype(F32), 64, 1).astype(BF16)

    def await_kv(parts):
        for part in parts:
            pair_kv_arrival(part).wait_recv()
            for way in range(2):
                passed(1, way, part).wait_recv()
                passed(2, way, part).wait_recv()

    many = jnp.ones((256, 128), BF16)
    half_masks = [
        jnp.where(low16, 1.0, 0.0).astype(BF16), jnp.where(low16, 0.0, 1.0).astype(BF16)
    ]
    masks = []
    for head in range(6):
        residue = lax.rem(6 * core + head, 8)
        masks.append(jnp.where(lane16 // 16 == residue, PENALTY, 0.0).astype(BF16))

    def stacked(value):
        return value.reshape(-1, 128)

    def left_side(block, slides, head):
        return jnp.concatenate(
            [stacked(block * half_masks[head % 2]), stacked((slides - 1) * masks[head])], 1
        )

    def levels(top, totals):
        return jnp.where(top < -PENALTY / 2, ABSENT, top + jnp.log(totals))

    def in_pieces(level):
        high = level.astype(BF16).astype(F32)
        rest = level - high
        middle = rest.astype(BF16).astype(F32)
        last = rest - middle
        at = lax.rem(lanes_of(level.shape), 8)
        pieces = jnp.where(
            at == 0, high, jnp.where(at == 1, middle, jnp.where(at == 2, last, 0.0))
        )
        return pieces.astype(BF16)

    def keys_of(part, j):
        slides = kv_roll[...] if part else kv[:, 0]
        return jnp.concatenate([stacked(kv[:, 1 + 6 * part + 2 * j]), stacked(slides)], 1)

    def values_of(part, j):
        return jnp.concatenate([stacked(kv[:, 2 + 6 * part + 2 * j]), many], 1)

    def inside(first, count):
        rows = count * 32
        span = pl.ds(first, count)
        low = lanes_of((rows, 128)) < HDIM
        spot = lanes_of((rows, 128)) // 8
        stats = jnp.zeros((rows, 128), F32)
        slides, turned = q_in[span, :, 0], q_roll[span]
        for j in range(3):
            far_q, near_q = q_in[span, :, 1 + j], q_in[span, :, 4 + j]
            lhs = jnp.concatenate(
                [
                    left_side(far_q, slides, 2 * j), left_side(near_q, turned, 2 * j),
                    left_side(far_q, slides, 2 * j + 1), left_side(near_q, turned, 2 * j + 1),
                ],
                0,
            )
            far_s, near_s = nt_dot(lhs, keys_of(0, j)), nt_dot(lhs, keys_of(1, j))
            top = jnp.max(jnp.maximum(far_s, near_s), axis=1, keepdims=True)
            far_o = nn_dot(jnp.exp(far_s - top).astype(BF16), values_of(0, j))
            both = far_o + nn_dot(jnp.exp(near_s - top).astype(BF16), values_of(1, j))
            for part in range(2):
                outs = []
                for u in range(2):
                    start = (2 * u + part) * rows
                    total = both[start:start + rows]
                    if part == 0:
                        total = total + far_o[start:start + rows]
                    outs.append(total[:, :128] / total[:, 128:])
                    level = levels(top[start:start + rows], total[:, 128:])
                    stats = jnp.where(spot == 8 * part + 2 * j + u, level, stats)
                o_in[span, :, 1 + 3 * part + j] = (
                    jnp.where(low, outs[0], outs[1]).astype(BF16).reshape(count, 2, 16, 128)
                )
        o_in[span, :, 0] = in_pieces(stats).reshape(count, 2, 16, 128)

    def outside(first, count):
        rows = count * 32
        span = pl.ds(first, count)
        low = lanes_of((rows, 128)) < HDIM
        spot = lanes_of((rows, 128)) // 8
        stats = jnp.zeros((rows, 128), F32)
        slides = q_out[span, :, 0]
        for j in range(3):
            far_q = q_out[span, :, 1 + j]
            lhs = jnp.concatenate(
                [left_side(far_q, slides, 2 * j), left_side(far_q, slides, 2 * j + 1)], 0
            )
            far_s = nt_dot(lhs, keys_of(0, j))
            top = jnp.max(far_s, axis=1, keepdims=True)
            total = nn_dot(jnp.exp(far_s - top).astype(BF16), values_of(0, j))
            result = total[:, :128] / total[:, 128:]
            level = levels(top, total[:, 128:])
            for u in range(2):
                stats = jnp.where(spot == 2 * j + u, level[u * rows:(u + 1) * rows], stats)
            o_out[span, :, 1 + j] = (
                jnp.where(low, result[:rows], result[rows:]).astype(BF16).reshape(count, 2, 16, 128)
            )
        o_out[span, :, 0] = in_pieces(stats).reshape(count, 2, 16, 128)

    def back_in(at, side):
        return pltpu.make_async_remote_copy(
            o_in.at[at, side], r_in.at[place, core], o_send_in.at[at, side],
            o_recv_in.at[place, core],
            device_id=(g - place + at, n - core + side), device_id_type=MESH,
        )

    def back_out(slot, side):
        at = lax.rem(slot + (place < 7).astype(jnp.int32) + place + 1, SEG)
        away = jnp.where(at > place, -SEG, SEG)
        other = lax.rem(g - place + at + away + WIDE, WIDE)
        return pltpu.make_async_remote_copy(
            o_out.at[slot, side], r_out.at[out_slot(place, at), core], o_send_out.at[slot, side],
            o_recv_out.at[out_slot(place, at), core],
            device_id=(other, n - core + side), device_id_type=MESH,
        )

    def if_near(at, act):
        apart = jnp.abs(at - place)

        @pl.when(jnp.logical_and(apart > 0, apart <= REACH))
        def _():
            for side in range(2):
                act(at, side)

    def if_used(slot, act):
        @pl.when(jnp.logical_or(slot < 5, lax.rem(place, 7) == 0))
        def _():
            for side in range(2):
                act(slot, side)

    await_kv((0, 1))

    @pl.loop(0, 2)
    def _(chunk):
        outside(3 * chunk, 3)
        for k in range(3):
            if_used(3 * chunk + k, lambda slot, side: back_out(slot, side).start())

    for slot in range(16):
        kv_roll[slot] = pltpu.roll(kv[slot, 0].astype(F32), 64, 1).astype(BF16)
    await_kv((2, 3))

    @pl.loop(0, SEG // SLOTS)
    def _(chunk):
        inside(SLOTS * chunk, SLOTS)
        for k in range(SLOTS):
            if_near(SLOTS * chunk + k, lambda at, side: back_in(at, side).start())

    pair_o = pltpu.make_async_remote_copy(
        o_in.at[place, 1 - core], r_in.at[place, core], pair_send.at[1], pair_recv.at[1],
        device_id=pair, device_id_type=MESH,
    )
    pair_o.start()
    r_in[place, core] = o_in[place, core]
    att[...] = loc_o[...]
    pair_q.wait_send()
    for part, way in both_ways:
        for side in range(2):
            first_kv(way, part, side).wait_send()
        if way == 1:
            pair_kv(part).wait_send()
        for kind in range(3):
            passed(kind, way, part).wait_send()
    for_partners(lambda i, side, inside: q_copy(i, side, inside).wait_send())

    @pl.loop(0, PARTNERS)
    def _(i):
        other, other_at, same = partner(i)

        @pl.when(same)
        def _():
            for side in range(2):
                spot = r_in.at[other_at, side]
                pltpu.make_async_copy(spot, spot, o_recv_in.at[other_at, side]).wait()

        @pl.when(jnp.logical_not(same))
        def _():
            slot = out_slot(other_at, place)
            for side in range(2):
                spot = r_out.at[slot, side]
                pltpu.make_async_copy(spot, spot, o_recv_out.at[slot, side]).wait()

    pair_o.wait_recv()

    e_row = lax.broadcasted_iota(jnp.int32, (128, 384), 0)
    e_col = lax.broadcasted_iota(jnp.int32, (128, 384), 1)
    to_far = jnp.where((e_row // 8 == e_col // 64) & (e_row % 8 < 3), 1.0, 0.0).astype(BF16)
    to_near = jnp.where((e_row // 8 == e_col // 64 + 8) & (e_row % 8 < 3), 1.0, 0.0).astype(BF16)
    for half in range(2):
        stats_i = r_in[:, half, 0].reshape(128, 128)
        stats_o = r_out[:, half, 0].reshape(96, 128)
        far_i = nn_dot(stats_i, to_far)
        near_i = nn_dot(stats_i, to_near)
        far_o = nn_dot(stats_o, to_far)
        for j in range(3):
            a = 3 * half + j
            lanes = slice(j * 128, (j + 1) * 128)
            cols = slice(a * 128, (a + 1) * 128)
            for part in range(2):
                r0 = (2 * a + 4 * part) % 8 * 16
                r1 = r0 + 16
                own_l = jnp.where(low16, loc_l[r0:r0 + 16, cols], loc_l[r1:r1 + 16, cols])
                own_o = jnp.where(low16, loc_o[r0:r0 + 16, cols], loc_o[r1:r1 + 16, cols])
                lev = (near_i if part else far_i)[:, lanes].reshape(8, 16, 128)
                val = r_in[:, half, 1 + 3 * part + j].astype(F32)
                if part == 0:
                    lev = jnp.concatenate([lev, far_o[:, lanes].reshape(6, 16, 128)], 0)
                    val = jnp.concatenate([val, r_out[:, half, 1 + j].astype(F32)], 0)
                top = jnp.maximum(jnp.max(lev, axis=0), own_l)
                scale = jnp.exp(lev - top[None])
                own_scale = jnp.exp(own_l - top)
                numer = jnp.sum(scale * val, axis=0) + own_scale * own_o
                denom = jnp.sum(scale, axis=0) + own_scale
                joined = numer / denom
                att[r0:r0 + 16, a * 128:a * 128 + 64] = joined[:, :64]
                att[r1:r1 + 16, a * 128 + 64:a * 128 + 128] = joined[:, 64:]

    back = (row == 8 * (col % 16) + col // 16).astype(F32).astype(BF16)
    attended = nn_dot(back, att[...].astype(BF16)).astype(BF16)
    loads[4].wait()
    out_ref[...] = nn_dot(attended, w_vmem[...]).astype(BF16)

    pair_o.wait_send()

    @pl.loop(0, 6)
    def _(slot):
        if_used(slot, lambda slot, side: back_out(slot, side).wait_send())

    @pl.loop(0, SEG)
    def _(at):
        if_near(at, lambda at, side: back_in(at, side).wait_send())


def local(queries, keys, values, slide_ids, w_out):
    vmem = pl.BlockSpec(memory_space=pltpu.VMEM)
    dma = pltpu.SemaphoreType.DMA
    return pl.pallas_call(
        kernel,
        out_shape=jax.ShapeDtypeStruct((TOK, WIDTH), BF16),
        in_specs=[pl.BlockSpec(memory_space=pltpu.HBM)] * 5,
        out_specs=vmem,
        scratch_shapes=[
            pltpu.VMEM((TOK, WIDTH), BF16),
            pltpu.VMEM((TOK, WIDTH), BF16),
            pltpu.VMEM((TOK, WIDTH), BF16),
            pltpu.VMEM((1, TOK), jnp.int32),
            pltpu.VMEM((TOK, WIDTH), BF16),
            pltpu.VMEM((TOK, WIDTH), BF16),
            pltpu.VMEM((TOK, WIDTH), BF16),
            pltpu.VMEM((TOK, 128), BF16),
            pltpu.VMEM((2, 13, 16, 128), BF16),
            pltpu.VMEM((2, 7, 16, 128), BF16),
            pltpu.VMEM((16, 13, 16, 128), BF16),
            pltpu.VMEM((16, 16, 128), BF16),
            pltpu.VMEM((8, 2, 7, 16, 128), BF16),
            pltpu.VMEM((6, 2, 4, 16, 128), BF16),
            pltpu.VMEM((8, 2, 16, 128), BF16),
            pltpu.VMEM((8, 2, 7, 16, 128), BF16),
            pltpu.VMEM((6, 2, 4, 16, 128), BF16),
            pltpu.VMEM((8, 2, 7, 16, 128), BF16),
            pltpu.VMEM((6, 2, 4, 16, 128), BF16),
            pltpu.VMEM((TOK, WIDTH), F32),
            pltpu.VMEM((TOK, WIDTH), F32),
            pltpu.VMEM((TOK, WIDTH), F32),
            pltpu.VMEM((WIDTH, WIDTH), BF16),
            dma((5,)),
            dma((2,)),
            dma((2,)),
            dma((11 * PARTS,)),
            dma((16 * PARTS,)),
            dma((24,)),
            dma((8, 2)),
            dma((6, 2)),
            dma((8, 2)),
            dma((6, 2)),
            dma((8, 2)),
            dma((6, 2)),
        ],
        compiler_params=pltpu.CompilerParams(
            collective_id=0, has_side_effects=True, vmem_limit_bytes=(63 * 1024 + 512) * 1024
        ),
        name="dilated",
    )(queries, keys, values, slide_ids.reshape(1, TOK), w_out)


def solution(mesh):
    placed = (
        P(("wide", "narrow"), None),
        P(("wide", "narrow"), None),
        P(("wide", "narrow"), None),
        P(("wide", "narrow")),
        P(),
    )
    return jax.shard_map(
        local, mesh=mesh, in_specs=placed, out_specs=P(("wide", "narrow"), None), check_vma=False
    )
```

```python
import jax
import jax.numpy as jnp
from jax import lax
from jax.experimental import pallas as pl
from jax.experimental.pallas import tpu as pltpu
from jax.sharding import PartitionSpec as P

MESH = pl.DeviceIdType.MESH
HEADS = 12
HDIM = 64
WIDTH = 768
TOK = 128
WIDE = 32
SEG = 8
REACH = 6
PARTNERS = 2 * REACH
PENALTY = 2048.0
ABSENT = -1e30
BF16 = jnp.bfloat16
F32 = jnp.float32

KV_PARTS = ((0, 4), (4, 3), (7, 3), (10, 3))
PARTS = len(KV_PARTS)
SLOTS = 2


def lanes_of(shape):
    return lax.broadcasted_iota(jnp.int32, shape, len(shape) - 1)


def nt_dot(left, right):
    return lax.dot_general(left, right, (((1,), (1,)), ((), ())), preferred_element_type=F32)


def nn_dot(left, right):
    return lax.dot_general(left, right, (((1,), (0,)), ((), ())), preferred_element_type=F32)


def out_slot(sender_at, receiver_at):
    return lax.rem(sender_at - receiver_at + 15, 8) - (receiver_at < 7).astype(jnp.int32)


def kernel(
    q_hbm, k_hbm, v_hbm, ids_hbm, w_hbm, out_ref,
    q_ref, k_ref, v_ref, ids_ref,
    pq, pk, pv, pc, kv_sel, q_sel, kv, kv_roll, q_in, q_out, q_roll, o_in, o_out, r_in, r_out,
    loc_o, loc_l, att, w_vmem,
    in_sem, pair_send, pair_recv, ring_send, ring_recv,
    q_send, q_recv_in, q_recv_out, o_send_in, o_send_out, o_recv_in, o_recv_out,
):
    g = lax.axis_index("wide")
    n = lax.axis_index("narrow")
    place = lax.rem(g, SEG)
    core = lax.rem(n, 2)
    pair = (g, n + 1 - 2 * core)
    right = (g, lax.rem(n + 2, 16))
    left = (g, lax.rem(n + 14, 16))
    right2 = (g, lax.rem(n + 4, 16))
    left2 = (g, lax.rem(n + 12, 16))

    def partner(i):
        offset = i - REACH + (i >= REACH).astype(jnp.int32)
        other = lax.rem(g + offset + WIDE, WIDE)
        return other, lax.rem(other, SEG), other // SEG == g // SEG

    empty = jnp.where(lax.rem(lanes_of((2, 16, 128)), 8) == 0, ABSENT, 0.0).astype(BF16)
    spare = SEG - 1 - place
    r_in[spare] = jnp.zeros((2, 7, 16, 128), BF16)
    r_in[spare, :, 0] = empty
    r_out[5] = jnp.zeros((2, 4, 16, 128), BF16)
    r_out[5, :, 0] = empty

    loads = [
        pltpu.make_async_copy(source, target, in_sem.at[at])
        for at, (source, target) in enumerate(
            ((ids_hbm, ids_ref), (k_hbm, k_ref), (v_hbm, v_ref), (q_hbm, q_ref), (w_hbm, w_vmem))
        )
    ]
    for load in loads[:4]:
        load.start()

    barrier = pltpu.get_barrier_semaphore()
    turn = 1 - 2 * core
    crossed = ((g, right[1] + turn), (g, left[1] + turn))
    for device in (pair, right, left, right2, left2) + crossed:
        pl.semaphore_signal(barrier, inc=1, device_id=device, device_id_type=MESH)

    for apart in range(-REACH, REACH + 1):
        if apart:
            for side in range(2):
                pl.semaphore_signal(
                    barrier, inc=1, device_id_type=MESH,
                    device_id=(lax.rem(g + apart + WIDE, WIDE), n - core + side),
                )

    row = lax.broadcasted_iota(jnp.int32, (TOK, TOK), 0)
    col = lax.broadcasted_iota(jnp.int32, (TOK, TOK), 1)
    order = (col == 8 * (row % 16) + row // 16).astype(F32).astype(BF16)
    loads[0].wait()
    unlike = (jnp.broadcast_to(ids_ref[...], (TOK, TOK)) != row % 16).astype(F32).astype(BF16)
    sorted_c = nt_dot(order, unlike)
    pc[...] = sorted_c.astype(BF16)
    lane16 = lanes_of((16, 128))
    low16 = lane16 < HDIM
    others = jnp.zeros((16, 128), F32)
    for residue in range(8):
        others = jnp.where(
            lane16 // 16 == residue, sorted_c[residue * 16:residue * 16 + 16], others
        )
    others = others.astype(BF16)
    for half in range(2):
        kv_sel[half, 0] = others
        q_sel[half, 0] = others

    def picked(source, a, shift):
        first = (2 * a + shift) % 8
        block = source[:, a * 128:(a + 1) * 128]
        return jnp.where(
            low16, block[first * 16:first * 16 + 16], block[first * 16 + 16:first * 16 + 32]
        ).astype(BF16)

    loads[1].wait()
    sorted_k = nn_dot(order, k_ref[...])
    pk[...] = sorted_k.astype(BF16)
    for a in range(6):
        for part in range(2):
            kv_sel[a // 3, 1 + 2 * (a % 3) + 6 * part] = picked(sorted_k, a, 4 * part)
    loads[2].wait()
    sorted_v = nn_dot(order, v_ref[...])
    pv[...] = sorted_v.astype(BF16)
    for a in range(6):
        for part in range(2):
            kv_sel[a // 3, 2 + 2 * (a % 3) + 6 * part] = picked(sorted_v, a, 4 * part)
    kv[core] = kv_sel[core]
    pl.semaphore_wait(barrier, 7 + 2 * PARTNERS)

    def send(source, target, sent, arrived, device):
        return pltpu.make_async_remote_copy(
            source, target, ring_send.at[sent], ring_recv.at[arrived],
            device_id=device, device_id_type=MESH,
        )

    def pair_kv(part):
        first, count = KV_PARTS[part]
        rows = pl.ds(first, count)
        return send(
            kv_sel.at[1 - core, rows], kv.at[core, rows], part, core * PARTS + part, pair
        )

    def pair_kv_arrival(part):
        first, count = KV_PARTS[part]
        rows = pl.ds(first, count)
        other = 1 - core
        return send(kv_sel.at[core, rows], kv.at[other, rows], part, other * PARTS + part, pair)

    def first_kv(way, part, side):
        first, count = KV_PARTS[part]
        rows = pl.ds(first, count)
        slot = (2, 14)[way] + core
        device = (g, lax.rem(n - core + (2, 14)[way], 16) + side)
        return send(
            kv_sel.at[side, rows], kv.at[slot, rows],
            PARTS + (way * PARTS + part) * 2 + side, slot * PARTS + part, device,
        )

    def first_arrival(way, part, side):
        first, count = KV_PARTS[part]
        rows = pl.ds(first, count)
        slot = (2, 14)[way] + side
        return send(
            kv_sel.at[0, rows], kv.at[slot, rows],
            PARTS + (way * PARTS + part) * 2 + side, slot * PARTS + part, pair,
        )

    def passed(kind, way, part):
        first, count = KV_PARTS[part]
        rows = pl.ds(first, count)
        at, to = (((2, 4), (4, 6), (4, 8)), ((14, 12), (12, 10), (13, 9)))[way][kind]
        slots = 1 if kind == 2 else 2
        device = ((right, right, right2), (left, left, left2))[way][kind]
        return send(
            kv.at[pl.ds(at, slots), rows], kv.at[pl.ds(to, slots), rows],
            5 * PARTS + (kind * 2 + way) * PARTS + part, to * PARTS + part, device,
        )

    both_ways = [(part, way) for part in range(PARTS) for way in range(2)]
    for part, way in both_ways:
        for side in range(2):
            first_kv(way, part, side).start()
        if way == 1:
            pair_kv(part).start()
    loads[3].wait()
    sorted_q = nn_dot(order, q_ref[...]) * (HDIM ** -0.5)
    pq[...] = sorted_q.astype(BF16)
    for a in range(6):
        for part in range(2):
            q_sel[a // 3, 1 + 3 * part + a % 3] = picked(sorted_q, a, 4 * part)
    q_in[place, core] = q_sel[core]
    loads[4].start()

    pair_q = pltpu.make_async_remote_copy(
        q_sel.at[1 - core], q_in.at[place, core], pair_send.at[0], pair_recv.at[0],
        device_id=pair, device_id_type=MESH,
    )
    pair_q.start()

    def pass_on(stage):
        for part, way in both_ways:
            if stage == 0:
                for side in range(2):
                    first_arrival(way, part, side).wait_recv()
                passed(0, way, part).start()
            else:
                passed(0, way, part).wait_recv()
                passed(1, way, part).start()
                passed(2, way, part).start()

    def q_copy(i, side, inside):
        other, other_at, _ = partner(i)
        if inside:
            source, target, arrived = q_sel.at[side], q_in.at[place, core], q_recv_in.at[place, core]
        else:
            slot = out_slot(place, other_at)
            source, target = q_sel.at[side, pl.ds(0, 4)], q_out.at[slot, core]
            arrived = q_recv_out.at[slot, core]
        return pltpu.make_async_remote_copy(
            source, target, q_send.at[2 * i + side], arrived,
            device_id=(other, n - core + side), device_id_type=MESH,
        )

    def for_partners(act):
        @pl.loop(0, PARTNERS)
        def _(i):
            _, _, same = partner(i)

            @pl.when(same)
            def _():
                for side in range(2):
                    act(i, side, True)

            @pl.when(jnp.logical_not(same))
            def _():
                for side in range(2):
                    act(i, side, False)

    for_partners(lambda i, side, inside: q_copy(i, side, inside).start())

    ones = jnp.ones((TOK, 128), BF16)
    lane128 = lanes_of((TOK, 128))
    own_slide = jnp.where(lane128 < 16, (sorted_c - 1.0) * PENALTY, 0.0).astype(BF16)
    wide_low = lanes_of((TOK, 128)) < HDIM

    def local_pair(a):
        cols = slice(a * 128, (a + 1) * 128)
        block = pq[:, cols].astype(F32)
        left_side = jnp.concatenate(
            [
                jnp.concatenate([jnp.where(wide_low, block, 0.0).astype(BF16), own_slide], 1),
                jnp.concatenate([jnp.where(wide_low, 0.0, block).astype(BF16), own_slide], 1),
            ],
            0,
        )
        scores = nt_dot(left_side, jnp.concatenate([pk[:, cols], pc[...]], 1))
        top = jnp.max(scores, axis=1, keepdims=True)
        weights = jnp.exp(scores - top).astype(BF16)
        summed = nn_dot(weights, jnp.concatenate([pv[:, cols], ones], 1))
        result = summed[:, :128] / summed[:, 128:]
        level = top + jnp.log(summed[:, 128:])
        loc_o[:, cols] = jnp.where(wide_low, result[:TOK], result[TOK:])
        loc_l[:, cols] = jnp.where(wide_low, level[:TOK], level[TOK:])

    local_pair(0)
    local_pair(1)
    pass_on(0)
    local_pair(2)
    local_pair(3)
    pass_on(1)
    local_pair(4)
    local_pair(5)

    pair_q.wait_recv()

    @pl.loop(0, PARTNERS)
    def _(i):
        other, other_at, same = partner(i)

        @pl.when(same)
        def _():
            for side in range(2):
                spot = q_in.at[other_at, side]
                pltpu.make_async_copy(spot, spot, q_recv_in.at[other_at, side]).wait()

        @pl.when(jnp.logical_not(same))
        def _():
            slot = out_slot(other_at, place)
            for side in range(2):
                spot = q_out.at[slot, side]
                pltpu.make_async_copy(spot, spot, q_recv_out.at[slot, side]).wait()

    for side in range(2):
        for slot in range(SEG):
            q_roll[slot, side] = pltpu.roll(q_in[slot, side, 0].astype(F32), 64, 1).astype(BF16)

    def await_kv(parts):
        for part in parts:
            pair_kv_arrival(part).wait_recv()
            for way in range(2):
                passed(1, way, part).wait_recv()
                passed(2, way, part).wait_recv()

    many = jnp.ones((256, 128), BF16)
    half_masks = [
        jnp.where(low16, 1.0, 0.0).astype(BF16), jnp.where(low16, 0.0, 1.0).astype(BF16)
    ]
    masks = []
    for head in range(6):
        residue = lax.rem(6 * core + head, 8)
        masks.append(jnp.where(lane16 // 16 == residue, PENALTY, 0.0).astype(BF16))

    def stacked(value):
        return value.reshape(-1, 128)

    def left_side(block, slides, head):
        return jnp.concatenate(
            [stacked(block * half_masks[head % 2]), stacked((slides - 1) * masks[head])], 1
        )

    def levels(top, totals):
        return jnp.where(top < -PENALTY / 2, ABSENT, top + jnp.log(totals))

    def in_pieces(level):
        high = level.astype(BF16).astype(F32)
        rest = level - high
        middle = rest.astype(BF16).astype(F32)
        last = rest - middle
        at = lax.rem(lanes_of(level.shape), 8)
        pieces = jnp.where(
            at == 0, high, jnp.where(at == 1, middle, jnp.where(at == 2, last, 0.0))
        )
        return pieces.astype(BF16)

    def keys_of(part, j):
        slides = kv_roll[...] if part else kv[:, 0]
        return jnp.concatenate([stacked(kv[:, 1 + 6 * part + 2 * j]), stacked(slides)], 1)

    def values_of(part, j):
        return jnp.concatenate([stacked(kv[:, 2 + 6 * part + 2 * j]), many], 1)

    def inside(first, count):
        rows = count * 32
        span = pl.ds(first, count)
        low = lanes_of((rows, 128)) < HDIM
        spot = lanes_of((rows, 128)) // 8
        stats = jnp.zeros((rows, 128), F32)
        slides, turned = q_in[span, :, 0], q_roll[span]
        for j in range(3):
            far_q, near_q = q_in[span, :, 1 + j], q_in[span, :, 4 + j]
            lhs = jnp.concatenate(
                [
                    left_side(far_q, slides, 2 * j), left_side(near_q, turned, 2 * j),
                    left_side(far_q, slides, 2 * j + 1), left_side(near_q, turned, 2 * j + 1),
                ],
                0,
            )
            far_s, near_s = nt_dot(lhs, keys_of(0, j)), nt_dot(lhs, keys_of(1, j))
            top = jnp.max(jnp.maximum(far_s, near_s), axis=1, keepdims=True)
            far_o = nn_dot(jnp.exp(far_s - top).astype(BF16), values_of(0, j))
            both = far_o + nn_dot(jnp.exp(near_s - top).astype(BF16), values_of(1, j))
            for part in range(2):
                outs = []
                for u in range(2):
                    start = (2 * u + part) * rows
                    total = both[start:start + rows]
                    if part == 0:
                        total = total + far_o[start:start + rows]
                    outs.append(total[:, :128] / total[:, 128:])
                    level = levels(top[start:start + rows], total[:, 128:])
                    stats = jnp.where(spot == 8 * part + 2 * j + u, level, stats)
                o_in[span, :, 1 + 3 * part + j] = (
                    jnp.where(low, outs[0], outs[1]).astype(BF16).reshape(count, 2, 16, 128)
                )
        o_in[span, :, 0] = in_pieces(stats).reshape(count, 2, 16, 128)

    def outside(first, count):
        rows = count * 32
        span = pl.ds(first, count)
        low = lanes_of((rows, 128)) < HDIM
        spot = lanes_of((rows, 128)) // 8
        stats = jnp.zeros((rows, 128), F32)
        slides = q_out[span, :, 0]
        for j in range(3):
            far_q = q_out[span, :, 1 + j]
            lhs = jnp.concatenate(
                [left_side(far_q, slides, 2 * j), left_side(far_q, slides, 2 * j + 1)], 0
            )
            far_s = nt_dot(lhs, keys_of(0, j))
            top = jnp.max(far_s, axis=1, keepdims=True)
            total = nn_dot(jnp.exp(far_s - top).astype(BF16), values_of(0, j))
            result = total[:, :128] / total[:, 128:]
            level = levels(top, total[:, 128:])
            for u in range(2):
                stats = jnp.where(spot == 2 * j + u, level[u * rows:(u + 1) * rows], stats)
            o_out[span, :, 1 + j] = (
                jnp.where(low, result[:rows], result[rows:]).astype(BF16).reshape(count, 2, 16, 128)
            )
        o_out[span, :, 0] = in_pieces(stats).reshape(count, 2, 16, 128)

    def back_in(at, side):
        return pltpu.make_async_remote_copy(
            o_in.at[at, side], r_in.at[place, core], o_send_in.at[at, side],
            o_recv_in.at[place, core],
            device_id=(g - place + at, n - core + side), device_id_type=MESH,
        )

    def back_out(slot, side):
        at = lax.rem(slot + (place < 7).astype(jnp.int32) + place + 1, SEG)
        away = jnp.where(at > place, -SEG, SEG)
        other = lax.rem(g - place + at + away + WIDE, WIDE)
        return pltpu.make_async_remote_copy(
            o_out.at[slot, side], r_out.at[out_slot(place, at), core], o_send_out.at[slot, side],
            o_recv_out.at[out_slot(place, at), core],
            device_id=(other, n - core + side), device_id_type=MESH,
        )

    def if_near(at, act):
        apart = jnp.abs(at - place)

        @pl.when(jnp.logical_and(apart > 0, apart <= REACH))
        def _():
            for side in range(2):
                act(at, side)

    def if_used(slot, act):
        @pl.when(jnp.logical_or(slot < 5, lax.rem(place, 7) == 0))
        def _():
            for side in range(2):
                act(slot, side)

    await_kv((0, 1))

    @pl.loop(0, 2)
    def _(chunk):
        outside(3 * chunk, 3)
        for k in range(3):
            if_used(3 * chunk + k, lambda slot, side: back_out(slot, side).start())

    for slot in range(16):
        kv_roll[slot] = pltpu.roll(kv[slot, 0].astype(F32), 64, 1).astype(BF16)
    await_kv((2, 3))

    @pl.loop(0, SEG // SLOTS)
    def _(step):
        chunk = lax.rem(step + place // SLOTS + 1, SEG // SLOTS)
        inside(SLOTS * chunk, SLOTS)
        for k in range(SLOTS):
            if_near(SLOTS * chunk + k, lambda at, side: back_in(at, side).start())

    pair_o = pltpu.make_async_remote_copy(
        o_in.at[place, 1 - core], r_in.at[place, core], pair_send.at[1], pair_recv.at[1],
        device_id=pair, device_id_type=MESH,
    )
    pair_o.start()
    r_in[place, core] = o_in[place, core]
    att[...] = loc_o[...]
    pair_q.wait_send()
    for part, way in both_ways:
        for side in range(2):
            first_kv(way, part, side).wait_send()
        if way == 1:
            pair_kv(part).wait_send()
        for kind in range(3):
            passed(kind, way, part).wait_send()
    for_partners(lambda i, side, inside: q_copy(i, side, inside).wait_send())

    @pl.loop(0, PARTNERS)
    def _(i):
        other, other_at, same = partner(i)

        @pl.when(same)
        def _():
            for side in range(2):
                spot = r_in.at[other_at, side]
                pltpu.make_async_copy(spot, spot, o_recv_in.at[other_at, side]).wait()

        @pl.when(jnp.logical_not(same))
        def _():
            slot = out_slot(other_at, place)
            for side in range(2):
                spot = r_out.at[slot, side]
                pltpu.make_async_copy(spot, spot, o_recv_out.at[slot, side]).wait()

    pair_o.wait_recv()

    e_row = lax.broadcasted_iota(jnp.int32, (128, 384), 0)
    e_col = lax.broadcasted_iota(jnp.int32, (128, 384), 1)
    to_far = jnp.where((e_row // 8 == e_col // 64) & (e_row % 8 < 3), 1.0, 0.0).astype(BF16)
    to_near = jnp.where((e_row // 8 == e_col // 64 + 8) & (e_row % 8 < 3), 1.0, 0.0).astype(BF16)
    for half in range(2):
        stats_i = r_in[:, half, 0].reshape(128, 128)
        stats_o = r_out[:, half, 0].reshape(96, 128)
        far_i = nn_dot(stats_i, to_far)
        near_i = nn_dot(stats_i, to_near)
        far_o = nn_dot(stats_o, to_far)
        for j in range(3):
            a = 3 * half + j
            lanes = slice(j * 128, (j + 1) * 128)
            cols = slice(a * 128, (a + 1) * 128)
            for part in range(2):
                r0 = (2 * a + 4 * part) % 8 * 16
                r1 = r0 + 16
                own_l = jnp.where(low16, loc_l[r0:r0 + 16, cols], loc_l[r1:r1 + 16, cols])
                own_o = jnp.where(low16, loc_o[r0:r0 + 16, cols], loc_o[r1:r1 + 16, cols])
                lev = (near_i if part else far_i)[:, lanes].reshape(8, 16, 128)
                val = r_in[:, half, 1 + 3 * part + j].astype(F32)
                if part == 0:
                    lev = jnp.concatenate([lev, far_o[:, lanes].reshape(6, 16, 128)], 0)
                    val = jnp.concatenate([val, r_out[:, half, 1 + j].astype(F32)], 0)
                top = jnp.maximum(jnp.max(lev, axis=0), own_l)
                scale = jnp.exp(lev - top[None])
                own_scale = jnp.exp(own_l - top)
                numer = jnp.sum(scale * val, axis=0) + own_scale * own_o
                denom = jnp.sum(scale, axis=0) + own_scale
                joined = numer / denom
                att[r0:r0 + 16, a * 128:a * 128 + 64] = joined[:, :64]
                att[r1:r1 + 16, a * 128 + 64:a * 128 + 128] = joined[:, 64:]

    back = (row == 8 * (col % 16) + col // 16).astype(F32).astype(BF16)
    attended = nn_dot(back, att[...].astype(BF16)).astype(BF16)
    loads[4].wait()
    out_ref[...] = nn_dot(attended, w_vmem[...]).astype(BF16)

    pair_o.wait_send()

    @pl.loop(0, 6)
    def _(slot):
        if_used(slot, lambda slot, side: back_out(slot, side).wait_send())

    @pl.loop(0, SEG)
    def _(at):
        if_near(at, lambda at, side: back_in(at, side).wait_send())


def local(queries, keys, values, slide_ids, w_out):
    vmem = pl.BlockSpec(memory_space=pltpu.VMEM)
    dma = pltpu.SemaphoreType.DMA
    return pl.pallas_call(
        kernel,
        out_shape=jax.ShapeDtypeStruct((TOK, WIDTH), BF16),
        in_specs=[pl.BlockSpec(memory_space=pltpu.HBM)] * 5,
        out_specs=vmem,
        scratch_shapes=[
            pltpu.VMEM((TOK, WIDTH), BF16),
            pltpu.VMEM((TOK, WIDTH), BF16),
            pltpu.VMEM((TOK, WIDTH), BF16),
            pltpu.VMEM((1, TOK), jnp.int32),
            pltpu.VMEM((TOK, WIDTH), BF16),
            pltpu.VMEM((TOK, WIDTH), BF16),
            pltpu.VMEM((TOK, WIDTH), BF16),
            pltpu.VMEM((TOK, 128), BF16),
            pltpu.VMEM((2, 13, 16, 128), BF16),
            pltpu.VMEM((2, 7, 16, 128), BF16),
            pltpu.VMEM((16, 13, 16, 128), BF16),
            pltpu.VMEM((16, 16, 128), BF16),
            pltpu.VMEM((8, 2, 7, 16, 128), BF16),
            pltpu.VMEM((6, 2, 4, 16, 128), BF16),
            pltpu.VMEM((8, 2, 16, 128), BF16),
            pltpu.VMEM((8, 2, 7, 16, 128), BF16),
            pltpu.VMEM((6, 2, 4, 16, 128), BF16),
            pltpu.VMEM((8, 2, 7, 16, 128), BF16),
            pltpu.VMEM((6, 2, 4, 16, 128), BF16),
            pltpu.VMEM((TOK, WIDTH), F32),
            pltpu.VMEM((TOK, WIDTH), F32),
            pltpu.VMEM((TOK, WIDTH), F32),
            pltpu.VMEM((WIDTH, WIDTH), BF16),
            dma((5,)),
            dma((2,)),
            dma((2,)),
            dma((11 * PARTS,)),
            dma((16 * PARTS,)),
            dma((24,)),
            dma((8, 2)),
            dma((6, 2)),
            dma((8, 2)),
            dma((6, 2)),
            dma((8, 2)),
            dma((6, 2)),
        ],
        compiler_params=pltpu.CompilerParams(
            collective_id=0, has_side_effects=True, vmem_limit_bytes=54960 * 1024
        ),
        name="dilated",
    )(queries, keys, values, slide_ids.reshape(1, TOK), w_out)


def solution(mesh):
    placed = (
        P(("wide", "narrow"), None),
        P(("wide", "narrow"), None),
        P(("wide", "narrow"), None),
        P(("wide", "narrow")),
        P(),
    )
    return jax.shard_map(
        local, mesh=mesh, in_specs=placed, out_specs=P(("wide", "narrow"), None), check_vma=False
    )
```

```python
import jax
import jax.numpy as jnp
from jax import lax
from jax.experimental import pallas as pl
from jax.experimental.pallas import tpu as pltpu
from jax.sharding import PartitionSpec as P

MESH = pl.DeviceIdType.MESH
HEADS = 12
HDIM = 64
WIDTH = 768
TOK = 128
WIDE = 32
SEG = 8
REACH = 6
PARTNERS = 2 * REACH
PENALTY = 2048.0
ABSENT = -1e30
BF16 = jnp.bfloat16
F32 = jnp.float32

KV_PARTS = ((0, 7), (7, 6))
PARTS = len(KV_PARTS)
SLOTS = 2


def lanes_of(shape):
    return lax.broadcasted_iota(jnp.int32, shape, len(shape) - 1)


def nt_dot(left, right):
    return lax.dot_general(left, right, (((1,), (1,)), ((), ())), preferred_element_type=F32)


def nn_dot(left, right):
    return lax.dot_general(left, right, (((1,), (0,)), ((), ())), preferred_element_type=F32)


def out_slot(sender_at, receiver_at):
    return lax.rem(sender_at - receiver_at + 15, 8) - (receiver_at < 7).astype(jnp.int32)


def kernel(
    q_hbm, k_hbm, v_hbm, ids_hbm, w_hbm, out_ref,
    q_ref, k_ref, v_ref, ids_ref,
    pq, pk, pv, pc, kv_sel, q_sel, kv, kv_roll, q_in, q_out, q_roll, o_in, o_out, r_in, r_out,
    loc_o, loc_l, att, w_vmem,
    in_sem, pair_send, pair_recv, ring_send, ring_recv,
    q_send, q_recv_in, q_recv_out, o_send_in, o_send_out, o_recv_in, o_recv_out,
):
    g = lax.axis_index("wide")
    n = lax.axis_index("narrow")
    place = lax.rem(g, SEG)
    core = lax.rem(n, 2)
    pair = (g, n + 1 - 2 * core)
    right = (g, lax.rem(n + 2, 16))
    left = (g, lax.rem(n + 14, 16))
    right2 = (g, lax.rem(n + 4, 16))
    left2 = (g, lax.rem(n + 12, 16))

    def partner(i):
        offset = i - REACH + (i >= REACH).astype(jnp.int32)
        other = lax.rem(g + offset + WIDE, WIDE)
        return other, lax.rem(other, SEG), other // SEG == g // SEG

    loads = [
        pltpu.make_async_copy(source, target, in_sem.at[at])
        for at, (source, target) in enumerate(
            ((ids_hbm, ids_ref), (k_hbm, k_ref), (v_hbm, v_ref), (q_hbm, q_ref), (w_hbm, w_vmem))
        )
    ]
    for load in loads[:4]:
        load.start()

    empty = jnp.where(lax.rem(lanes_of((2, 16, 128)), 8) == 0, ABSENT, 0.0).astype(BF16)
    spare = SEG - 1 - place
    r_in[spare] = jnp.zeros((2, 7, 16, 128), BF16)
    r_in[spare, :, 0] = empty
    r_out[5] = jnp.zeros((2, 4, 16, 128), BF16)
    r_out[5, :, 0] = empty

    barrier = pltpu.get_barrier_semaphore()
    turn = 1 - 2 * core
    crossed = ((g, right[1] + turn), (g, left[1] + turn))
    for device in (pair, right, left, right2, left2) + crossed:
        pl.semaphore_signal(barrier, inc=1, device_id=device, device_id_type=MESH)

    for apart in range(-REACH, REACH + 1):
        if apart:
            for side in range(2):
                pl.semaphore_signal(
                    barrier, inc=1, device_id_type=MESH,
                    device_id=(lax.rem(g + apart + WIDE, WIDE), n - core + side),
                )

    row = lax.broadcasted_iota(jnp.int32, (TOK, TOK), 0)
    col = lax.broadcasted_iota(jnp.int32, (TOK, TOK), 1)
    order = (col == 8 * (row % 16) + row // 16).astype(F32).astype(BF16)
    loads[0].wait()
    unlike = (jnp.broadcast_to(ids_ref[...], (TOK, TOK)) != row % 16).astype(F32).astype(BF16)
    sorted_c = nt_dot(order, unlike)
    pc[...] = sorted_c.astype(BF16)
    lane16 = lanes_of((16, 128))
    low16 = lane16 < HDIM
    others = jnp.zeros((16, 128), F32)
    for residue in range(8):
        others = jnp.where(
            lane16 // 16 == residue, sorted_c[residue * 16:residue * 16 + 16], others
        )
    others = others.astype(BF16)
    for half in range(2):
        kv_sel[half, 0] = others
        q_sel[half, 0] = others

    def picked(source, a, shift):
        first = (2 * a + shift) % 8
        block = source[:, a * 128:(a + 1) * 128]
        return jnp.where(
            low16, block[first * 16:first * 16 + 16], block[first * 16 + 16:first * 16 + 32]
        ).astype(BF16)

    loads[1].wait()
    sorted_k = nn_dot(order, k_ref[...])
    pk[...] = sorted_k.astype(BF16)
    for a in range(6):
        for part in range(2):
            kv_sel[a // 3, 1 + 2 * (a % 3) + 6 * part] = picked(sorted_k, a, 4 * part)
    loads[2].wait()
    sorted_v = nn_dot(order, v_ref[...])
    pv[...] = sorted_v.astype(BF16)
    for a in range(6):
        for part in range(2):
            kv_sel[a // 3, 2 + 2 * (a % 3) + 6 * part] = picked(sorted_v, a, 4 * part)
    kv[core] = kv_sel[core]
    pl.semaphore_wait(barrier, 7 + 2 * PARTNERS)

    def send(source, target, sent, arrived, device):
        return pltpu.make_async_remote_copy(
            source, target, ring_send.at[sent], ring_recv.at[arrived],
            device_id=device, device_id_type=MESH,
        )

    def pair_kv(part):
        first, count = KV_PARTS[part]
        rows = pl.ds(first, count)
        return send(
            kv_sel.at[1 - core, rows], kv.at[core, rows], part, core * PARTS + part, pair
        )

    def pair_kv_arrival(part):
        first, count = KV_PARTS[part]
        rows = pl.ds(first, count)
        other = 1 - core
        return send(kv_sel.at[core, rows], kv.at[other, rows], part, other * PARTS + part, pair)

    def first_kv(way, part, side):
        first, count = KV_PARTS[part]
        rows = pl.ds(first, count)
        slot = (2, 14)[way] + core
        device = (g, lax.rem(n - core + (2, 14)[way], 16) + side)
        return send(
            kv_sel.at[side, rows], kv.at[slot, rows],
            PARTS + (way * PARTS + part) * 2 + side, slot * PARTS + part, device,
        )

    def first_arrival(way, part, side):
        first, count = KV_PARTS[part]
        rows = pl.ds(first, count)
        slot = (2, 14)[way] + side
        return send(
            kv_sel.at[0, rows], kv.at[slot, rows],
            PARTS + (way * PARTS + part) * 2 + side, slot * PARTS + part, pair,
        )

    def passed(kind, way, part):
        first, count = KV_PARTS[part]
        rows = pl.ds(first, count)
        at, to = (((2, 4), (4, 6), (4, 8)), ((14, 12), (12, 10), (13, 9)))[way][kind]
        slots = 1 if kind == 2 else 2
        device = ((right, right, right2), (left, left, left2))[way][kind]
        return send(
            kv.at[pl.ds(at, slots), rows], kv.at[pl.ds(to, slots), rows],
            5 * PARTS + (kind * 2 + way) * PARTS + part, to * PARTS + part, device,
        )

    both_ways = [(part, way) for part in range(PARTS) for way in range(2)]
    for part, way in both_ways:
        for side in range(2):
            first_kv(way, part, side).start()
        if way == 1:
            pair_kv(part).start()
    loads[3].wait()
    sorted_q = nn_dot(order, q_ref[...]) * (HDIM ** -0.5)
    pq[...] = sorted_q.astype(BF16)
    for a in range(6):
        for part in range(2):
            q_sel[a // 3, 1 + 3 * part + a % 3] = picked(sorted_q, a, 4 * part)
    q_in[place, core] = q_sel[core]
    loads[4].start()

    pair_q = pltpu.make_async_remote_copy(
        q_sel.at[1 - core], q_in.at[place, core], pair_send.at[0], pair_recv.at[0],
        device_id=pair, device_id_type=MESH,
    )
    pair_q.start()

    def pass_on(stage):
        for part, way in both_ways:
            if stage == 0:
                for side in range(2):
                    first_arrival(way, part, side).wait_recv()
                passed(0, way, part).start()
            else:
                passed(0, way, part).wait_recv()
                passed(1, way, part).start()
                passed(2, way, part).start()

    def q_copy(i, side, inside):
        other, other_at, _ = partner(i)
        if inside:
            source, target, arrived = q_sel.at[side], q_in.at[place, core], q_recv_in.at[place, core]
        else:
            slot = out_slot(place, other_at)
            source, target = q_sel.at[side, pl.ds(0, 4)], q_out.at[slot, core]
            arrived = q_recv_out.at[slot, core]
        return pltpu.make_async_remote_copy(
            source, target, q_send.at[2 * i + side], arrived,
            device_id=(other, n - core + side), device_id_type=MESH,
        )

    def for_partners(act):
        @pl.loop(0, PARTNERS)
        def _(i):
            _, _, same = partner(i)

            @pl.when(same)
            def _():
                for side in range(2):
                    act(i, side, True)

            @pl.when(jnp.logical_not(same))
            def _():
                for side in range(2):
                    act(i, side, False)

    for_partners(lambda i, side, inside: q_copy(i, side, inside).start())

    ones = jnp.ones((TOK, 128), BF16)
    lane128 = lanes_of((TOK, 128))
    own_slide = jnp.where(lane128 < 16, (sorted_c - 1.0) * PENALTY, 0.0).astype(BF16)
    wide_low = lanes_of((TOK, 128)) < HDIM

    def local_pair(a):
        cols = slice(a * 128, (a + 1) * 128)
        block = pq[:, cols].astype(F32)
        left_side = jnp.concatenate(
            [
                jnp.concatenate([jnp.where(wide_low, block, 0.0).astype(BF16), own_slide], 1),
                jnp.concatenate([jnp.where(wide_low, 0.0, block).astype(BF16), own_slide], 1),
            ],
            0,
        )
        scores = nt_dot(left_side, jnp.concatenate([pk[:, cols], pc[...]], 1))
        top = jnp.max(scores, axis=1, keepdims=True)
        weights = jnp.exp(scores - top).astype(BF16)
        summed = nn_dot(weights, jnp.concatenate([pv[:, cols], ones], 1))
        result = summed[:, :128] / summed[:, 128:]
        level = top + jnp.log(summed[:, 128:])
        loc_o[:, cols] = jnp.where(wide_low, result[:TOK], result[TOK:])
        loc_l[:, cols] = jnp.where(wide_low, level[:TOK], level[TOK:])

    local_pair(0)
    local_pair(1)
    pass_on(0)
    local_pair(2)
    local_pair(3)
    pass_on(1)
    local_pair(4)
    local_pair(5)

    pair_q.wait_recv()

    @pl.loop(0, PARTNERS)
    def _(i):
        other, other_at, same = partner(i)

        @pl.when(same)
        def _():
            for side in range(2):
                spot = q_in.at[other_at, side]
                pltpu.make_async_copy(spot, spot, q_recv_in.at[other_at, side]).wait()

        @pl.when(jnp.logical_not(same))
        def _():
            slot = out_slot(other_at, place)
            for side in range(2):
                spot = q_out.at[slot, side]
                pltpu.make_async_copy(spot, spot, q_recv_out.at[slot, side]).wait()

    for side in range(2):
        for slot in range(SEG):
            q_roll[slot, side] = pltpu.roll(q_in[slot, side, 0].astype(F32), 64, 1).astype(BF16)

    def await_kv(parts):
        for part in parts:
            pair_kv_arrival(part).wait_recv()
            for way in range(2):
                passed(1, way, part).wait_recv()
                passed(2, way, part).wait_recv()

    many = jnp.ones((256, 128), BF16)
    half_masks = [
        jnp.where(low16, 1.0, 0.0).astype(BF16), jnp.where(low16, 0.0, 1.0).astype(BF16)
    ]
    masks = []
    for head in range(6):
        residue = lax.rem(6 * core + head, 8)
        masks.append(jnp.where(lane16 // 16 == residue, PENALTY, 0.0).astype(BF16))

    def stacked(value):
        return value.reshape(-1, 128)

    def left_side(block, slides, head):
        return jnp.concatenate(
            [stacked(block * half_masks[head % 2]), stacked((slides - 1) * masks[head])], 1
        )

    def levels(top, totals):
        return jnp.where(top < -PENALTY / 2, ABSENT, top + jnp.log(totals))

    def in_pieces(level):
        high = level.astype(BF16).astype(F32)
        rest = level - high
        middle = rest.astype(BF16).astype(F32)
        last = rest - middle
        at = lax.rem(lanes_of(level.shape), 8)
        pieces = jnp.where(
            at == 0, high, jnp.where(at == 1, middle, jnp.where(at == 2, last, 0.0))
        )
        return pieces.astype(BF16)

    def keys_of(part, j):
        slides = kv_roll[...] if part else kv[:, 0]
        return jnp.concatenate([stacked(kv[:, 1 + 6 * part + 2 * j]), stacked(slides)], 1)

    def values_of(part, j):
        return jnp.concatenate([stacked(kv[:, 2 + 6 * part + 2 * j]), many], 1)

    def inside(first, count):
        rows = count * 32
        span = pl.ds(first, count)
        low = lanes_of((rows, 128)) < HDIM
        spot = lanes_of((rows, 128)) // 8
        stats = jnp.zeros((rows, 128), F32)
        slides, turned = q_in[span, :, 0], q_roll[span]
        for j in range(3):
            far_q, near_q = q_in[span, :, 1 + j], q_in[span, :, 4 + j]
            lhs = jnp.concatenate(
                [
                    left_side(far_q, slides, 2 * j), left_side(near_q, turned, 2 * j),
                    left_side(far_q, slides, 2 * j + 1), left_side(near_q, turned, 2 * j + 1),
                ],
                0,
            )
            far_s, near_s = nt_dot(lhs, keys_of(0, j)), nt_dot(lhs, keys_of(1, j))
            top = jnp.max(jnp.maximum(far_s, near_s), axis=1, keepdims=True)
            far_o = nn_dot(jnp.exp(far_s - top).astype(BF16), values_of(0, j))
            both = far_o + nn_dot(jnp.exp(near_s - top).astype(BF16), values_of(1, j))
            for part in range(2):
                outs = []
                for u in range(2):
                    start = (2 * u + part) * rows
                    total = both[start:start + rows]
                    if part == 0:
                        total = total + far_o[start:start + rows]
                    outs.append(total[:, :128] / total[:, 128:])
                    level = levels(top[start:start + rows], total[:, 128:])
                    stats = jnp.where(spot == 8 * part + 2 * j + u, level, stats)
                o_in[span, :, 1 + 3 * part + j] = (
                    jnp.where(low, outs[0], outs[1]).astype(BF16).reshape(count, 2, 16, 128)
                )
        o_in[span, :, 0] = in_pieces(stats).reshape(count, 2, 16, 128)

    def outside(first, count):
        rows = count * 32
        span = pl.ds(first, count)
        low = lanes_of((rows, 128)) < HDIM
        spot = lanes_of((rows, 128)) // 8
        stats = jnp.zeros((rows, 128), F32)
        slides = q_out[span, :, 0]
        for j in range(3):
            far_q = q_out[span, :, 1 + j]
            lhs = jnp.concatenate(
                [left_side(far_q, slides, 2 * j), left_side(far_q, slides, 2 * j + 1)], 0
            )
            far_s = nt_dot(lhs, keys_of(0, j))
            top = jnp.max(far_s, axis=1, keepdims=True)
            total = nn_dot(jnp.exp(far_s - top).astype(BF16), values_of(0, j))
            result = total[:, :128] / total[:, 128:]
            level = levels(top, total[:, 128:])
            for u in range(2):
                stats = jnp.where(spot == 2 * j + u, level[u * rows:(u + 1) * rows], stats)
            o_out[span, :, 1 + j] = (
                jnp.where(low, result[:rows], result[rows:]).astype(BF16).reshape(count, 2, 16, 128)
            )
        o_out[span, :, 0] = in_pieces(stats).reshape(count, 2, 16, 128)

    def back_in(at, side):
        return pltpu.make_async_remote_copy(
            o_in.at[at, side], r_in.at[place, core], o_send_in.at[at, side],
            o_recv_in.at[place, core],
            device_id=(g - place + at, n - core + side), device_id_type=MESH,
        )

    def back_out(slot, side):
        at = lax.rem(slot + (place < 7).astype(jnp.int32) + place + 1, SEG)
        away = jnp.where(at > place, -SEG, SEG)
        other = lax.rem(g - place + at + away + WIDE, WIDE)
        return pltpu.make_async_remote_copy(
            o_out.at[slot, side], r_out.at[out_slot(place, at), core], o_send_out.at[slot, side],
            o_recv_out.at[out_slot(place, at), core],
            device_id=(other, n - core + side), device_id_type=MESH,
        )

    def if_near(at, act):
        apart = jnp.abs(at - place)

        @pl.when(jnp.logical_and(apart > 0, apart <= REACH))
        def _():
            for side in range(2):
                act(at, side)

    def if_used(slot, act):
        @pl.when(jnp.logical_or(slot < 5, lax.rem(place, 7) == 0))
        def _():
            for side in range(2):
                act(slot, side)

    await_kv((0,))

    outside(0, 6)

    @pl.loop(0, 6)
    def _(slot):
        if_used(slot, lambda slot, side: back_out(slot, side).start())

    for slot in range(16):
        kv_roll[slot] = pltpu.roll(kv[slot, 0].astype(F32), 64, 1).astype(BF16)
    await_kv((1,))

    @pl.loop(0, SEG // SLOTS)
    def _(step):
        chunk = lax.rem(step + place // SLOTS + 1, SEG // SLOTS)
        inside(SLOTS * chunk, SLOTS)
        for k in range(SLOTS):
            if_near(SLOTS * chunk + k, lambda at, side: back_in(at, side).start())

    pair_o = pltpu.make_async_remote_copy(
        o_in.at[place, 1 - core], r_in.at[place, core], pair_send.at[1], pair_recv.at[1],
        device_id=pair, device_id_type=MESH,
    )
    pair_o.start()
    r_in[place, core] = o_in[place, core]
    att[...] = loc_o[...]
    pair_q.wait_send()
    for part, way in both_ways:
        for side in range(2):
            first_kv(way, part, side).wait_send()
        if way == 1:
            pair_kv(part).wait_send()
        for kind in range(3):
            passed(kind, way, part).wait_send()
    for_partners(lambda i, side, inside: q_copy(i, side, inside).wait_send())

    pair_o.wait_send()

    @pl.loop(0, 6)
    def _(slot):
        if_used(slot, lambda slot, side: back_out(slot, side).wait_send())

    @pl.loop(0, SEG)
    def _(at):
        if_near(at, lambda at, side: back_in(at, side).wait_send())

    @pl.loop(0, PARTNERS)
    def _(i):
        other, other_at, same = partner(i)

        @pl.when(same)
        def _():
            for side in range(2):
                spot = r_in.at[other_at, side]
                pltpu.make_async_copy(spot, spot, o_recv_in.at[other_at, side]).wait()

        @pl.when(jnp.logical_not(same))
        def _():
            slot = out_slot(other_at, place)
            for side in range(2):
                spot = r_out.at[slot, side]
                pltpu.make_async_copy(spot, spot, o_recv_out.at[slot, side]).wait()

    pair_o.wait_recv()

    e_row = lax.broadcasted_iota(jnp.int32, (128, 384), 0)
    e_col = lax.broadcasted_iota(jnp.int32, (128, 384), 1)
    to_far = jnp.where((e_row // 8 == e_col // 64) & (e_row % 8 < 3), 1.0, 0.0).astype(BF16)
    to_near = jnp.where((e_row // 8 == e_col // 64 + 8) & (e_row % 8 < 3), 1.0, 0.0).astype(BF16)
    for half in range(2):
        stats_i = r_in[:, half, 0].reshape(128, 128)
        stats_o = r_out[:, half, 0].reshape(96, 128)
        far_i = nn_dot(stats_i, to_far)
        near_i = nn_dot(stats_i, to_near)
        far_o = nn_dot(stats_o, to_far)
        for j in range(3):
            a = 3 * half + j
            lanes = slice(j * 128, (j + 1) * 128)
            cols = slice(a * 128, (a + 1) * 128)
            for part in range(2):
                r0 = (2 * a + 4 * part) % 8 * 16
                r1 = r0 + 16
                own_l = jnp.where(low16, loc_l[r0:r0 + 16, cols], loc_l[r1:r1 + 16, cols])
                own_o = jnp.where(low16, loc_o[r0:r0 + 16, cols], loc_o[r1:r1 + 16, cols])
                lev = (near_i if part else far_i)[:, lanes].reshape(8, 16, 128)
                val = r_in[:, half, 1 + 3 * part + j].astype(F32)
                if part == 0:
                    lev = jnp.concatenate([lev, far_o[:, lanes].reshape(6, 16, 128)], 0)
                    val = jnp.concatenate([val, r_out[:, half, 1 + j].astype(F32)], 0)
                top = jnp.maximum(jnp.max(lev, axis=0), own_l)
                scale = jnp.exp(lev - top[None])
                own_scale = jnp.exp(own_l - top)
                numer = jnp.sum(scale * val, axis=0) + own_scale * own_o
                denom = jnp.sum(scale, axis=0) + own_scale
                joined = numer / denom
                att[r0:r0 + 16, a * 128:a * 128 + 64] = joined[:, :64]
                att[r1:r1 + 16, a * 128 + 64:a * 128 + 128] = joined[:, 64:]

    back = (row == 8 * (col % 16) + col // 16).astype(F32).astype(BF16)
    attended = nn_dot(back, att[...].astype(BF16)).astype(BF16)
    loads[4].wait()
    out_ref[...] = nn_dot(attended, w_vmem[...]).astype(BF16)


def local(queries, keys, values, slide_ids, w_out):
    vmem = pl.BlockSpec(memory_space=pltpu.VMEM)
    dma = pltpu.SemaphoreType.DMA
    return pl.pallas_call(
        kernel,
        out_shape=jax.ShapeDtypeStruct((TOK, WIDTH), BF16),
        in_specs=[pl.BlockSpec(memory_space=pltpu.HBM)] * 5,
        out_specs=vmem,
        scratch_shapes=[
            pltpu.VMEM((TOK, WIDTH), BF16),
            pltpu.VMEM((TOK, WIDTH), BF16),
            pltpu.VMEM((TOK, WIDTH), BF16),
            pltpu.VMEM((1, TOK), jnp.int32),
            pltpu.VMEM((TOK, WIDTH), BF16),
            pltpu.VMEM((TOK, WIDTH), BF16),
            pltpu.VMEM((TOK, WIDTH), BF16),
            pltpu.VMEM((TOK, 128), BF16),
            pltpu.VMEM((2, 13, 16, 128), BF16),
            pltpu.VMEM((2, 7, 16, 128), BF16),
            pltpu.VMEM((16, 13, 16, 128), BF16),
            pltpu.VMEM((16, 16, 128), BF16),
            pltpu.VMEM((8, 2, 7, 16, 128), BF16),
            pltpu.VMEM((6, 2, 4, 16, 128), BF16),
            pltpu.VMEM((8, 2, 16, 128), BF16),
            pltpu.VMEM((8, 2, 7, 16, 128), BF16),
            pltpu.VMEM((6, 2, 4, 16, 128), BF16),
            pltpu.VMEM((8, 2, 7, 16, 128), BF16),
            pltpu.VMEM((6, 2, 4, 16, 128), BF16),
            pltpu.VMEM((TOK, WIDTH), F32),
            pltpu.VMEM((TOK, WIDTH), F32),
            pltpu.VMEM((TOK, WIDTH), F32),
            pltpu.VMEM((WIDTH, WIDTH), BF16),
            dma((5,)),
            dma((2,)),
            dma((2,)),
            dma((11 * PARTS,)),
            dma((16 * PARTS,)),
            dma((24,)),
            dma((8, 2)),
            dma((6, 2)),
            dma((8, 2)),
            dma((6, 2)),
            dma((8, 2)),
            dma((6, 2)),
        ],
        compiler_params=pltpu.CompilerParams(
            collective_id=0, has_side_effects=True, vmem_limit_bytes=54960 * 1024
        ),
        name="dilated",
    )(queries, keys, values, slide_ids.reshape(1, TOK), w_out)


def solution(mesh):
    placed = (
        P(("wide", "narrow"), None),
        P(("wide", "narrow"), None),
        P(("wide", "narrow"), None),
        P(("wide", "narrow")),
        P(),
    )
    return jax.shard_map(
        local, mesh=mesh, in_specs=placed, out_specs=P(("wide", "narrow"), None), check_vma=False
    )
```

```python
import jax
import jax.numpy as jnp
from jax import lax
from jax.experimental import pallas as pl
from jax.experimental.pallas import tpu as pltpu
from jax.sharding import PartitionSpec as P

MESH = pl.DeviceIdType.MESH
HEADS = 12
HDIM = 64
WIDTH = 768
TOK = 128
WIDE = 32
SEG = 8
REACH = 6
PARTNERS = 2 * REACH
PENALTY = 2048.0
ABSENT = -1e30
BF16 = jnp.bfloat16
F32 = jnp.float32

KV_PARTS = ((0, 4), (4, 3), (7, 3), (10, 3))
PARTS = len(KV_PARTS)
SLOTS = 2


def lanes_of(shape):
    return lax.broadcasted_iota(jnp.int32, shape, len(shape) - 1)


def nt_dot(left, right):
    return lax.dot_general(left, right, (((1,), (1,)), ((), ())), preferred_element_type=F32)


def nn_dot(left, right):
    return lax.dot_general(left, right, (((1,), (0,)), ((), ())), preferred_element_type=F32)


def out_slot(sender_at, receiver_at):
    return lax.rem(sender_at - receiver_at + 15, 8) - (receiver_at < 7).astype(jnp.int32)


def kernel(
    q_hbm, k_hbm, v_hbm, ids_hbm, w_hbm, out_ref,
    q_ref, k_ref, v_ref, ids_ref,
    pq, pk, pv, pc, kv_sel, q_sel, kv, kv_roll, q_in, q_out, q_roll, o_in, o_out, r_in, r_out,
    loc_o, loc_l, att, w_vmem,
    in_sem, pair_send, pair_recv, ring_send, ring_recv,
    q_send, q_recv_in, q_recv_out, o_send_in, o_send_out, o_recv_in, o_recv_out,
):
    g = lax.axis_index("wide")
    n = lax.axis_index("narrow")
    place = lax.rem(g, SEG)
    core = lax.rem(n, 2)
    pair = (g, n + 1 - 2 * core)
    right = (g, lax.rem(n + 2, 16))
    left = (g, lax.rem(n + 14, 16))
    right2 = (g, lax.rem(n + 4, 16))
    left2 = (g, lax.rem(n + 12, 16))

    def partner(i):
        offset = i - REACH + (i >= REACH).astype(jnp.int32)
        other = lax.rem(g + offset + WIDE, WIDE)
        return other, lax.rem(other, SEG), other // SEG == g // SEG

    loads = [
        pltpu.make_async_copy(source, target, in_sem.at[at])
        for at, (source, target) in enumerate(
            ((ids_hbm, ids_ref), (k_hbm, k_ref), (v_hbm, v_ref), (q_hbm, q_ref), (w_hbm, w_vmem))
        )
    ]
    for load in loads[:4]:
        load.start()

    empty = jnp.where(lax.rem(lanes_of((2, 16, 128)), 8) == 0, ABSENT, 0.0).astype(BF16)
    spare = SEG - 1 - place
    r_in[spare] = jnp.zeros((2, 7, 16, 128), BF16)
    r_in[spare, :, 0] = empty
    r_out[5] = jnp.zeros((2, 4, 16, 128), BF16)
    r_out[5, :, 0] = empty

    barrier = pltpu.get_barrier_semaphore()
    turn = 1 - 2 * core
    crossed = ((g, right[1] + turn), (g, left[1] + turn))
    for device in (pair, right, left, right2, left2) + crossed:
        pl.semaphore_signal(barrier, inc=1, device_id=device, device_id_type=MESH)

    for apart in range(-REACH, REACH + 1):
        if apart:
            for side in range(2):
                pl.semaphore_signal(
                    barrier, inc=1, device_id_type=MESH,
                    device_id=(lax.rem(g + apart + WIDE, WIDE), n - core + side),
                )

    row = lax.broadcasted_iota(jnp.int32, (TOK, TOK), 0)
    col = lax.broadcasted_iota(jnp.int32, (TOK, TOK), 1)
    order = (col == 8 * (row % 16) + row // 16).astype(F32).astype(BF16)
    loads[0].wait()
    unlike = (jnp.broadcast_to(ids_ref[...], (TOK, TOK)) != row % 16).astype(F32).astype(BF16)
    sorted_c = nt_dot(order, unlike)
    pc[...] = sorted_c.astype(BF16)
    lane16 = lanes_of((16, 128))
    low16 = lane16 < HDIM
    others = jnp.zeros((16, 128), F32)
    for residue in range(8):
        others = jnp.where(
            lane16 // 16 == residue, sorted_c[residue * 16:residue * 16 + 16], others
        )
    others = others.astype(BF16)
    for half in range(2):
        kv_sel[half, 0] = others
        q_sel[half, 0] = others

    def picked(source, a, shift):
        first = (2 * a + shift) % 8
        block = source[:, a * 128:(a + 1) * 128]
        return jnp.where(
            low16, block[first * 16:first * 16 + 16], block[first * 16 + 16:first * 16 + 32]
        ).astype(BF16)

    loads[1].wait()
    sorted_k = nn_dot(order, k_ref[...])
    pk[...] = sorted_k.astype(BF16)
    for a in range(6):
        for part in range(2):
            kv_sel[a // 3, 1 + 2 * (a % 3) + 6 * part] = picked(sorted_k, a, 4 * part)
    loads[2].wait()
    sorted_v = nn_dot(order, v_ref[...])
    pv[...] = sorted_v.astype(BF16)
    for a in range(6):
        for part in range(2):
            kv_sel[a // 3, 2 + 2 * (a % 3) + 6 * part] = picked(sorted_v, a, 4 * part)
    kv[core] = kv_sel[core]
    pl.semaphore_wait(barrier, 7 + 2 * PARTNERS)

    def send(source, target, sent, arrived, device):
        return pltpu.make_async_remote_copy(
            source, target, ring_send.at[sent], ring_recv.at[arrived],
            device_id=device, device_id_type=MESH,
        )

    def pair_kv(part):
        first, count = KV_PARTS[part]
        rows = pl.ds(first, count)
        return send(
            kv_sel.at[1 - core, rows], kv.at[core, rows], part, core * PARTS + part, pair
        )

    def pair_kv_arrival(part):
        first, count = KV_PARTS[part]
        rows = pl.ds(first, count)
        other = 1 - core
        return send(kv_sel.at[core, rows], kv.at[other, rows], part, other * PARTS + part, pair)

    def first_kv(way, part, side):
        first, count = KV_PARTS[part]
        rows = pl.ds(first, count)
        slot = (2, 14)[way] + core
        device = (g, lax.rem(n - core + (2, 14)[way], 16) + side)
        return send(
            kv_sel.at[side, rows], kv.at[slot, rows],
            PARTS + (way * PARTS + part) * 2 + side, slot * PARTS + part, device,
        )

    def first_arrival(way, part, side):
        first, count = KV_PARTS[part]
        rows = pl.ds(first, count)
        slot = (2, 14)[way] + side
        return send(
            kv_sel.at[0, rows], kv.at[slot, rows],
            PARTS + (way * PARTS + part) * 2 + side, slot * PARTS + part, pair,
        )

    def passed(kind, way, part):
        first, count = KV_PARTS[part]
        rows = pl.ds(first, count)
        at, to = (((2, 4), (4, 6), (4, 8)), ((14, 12), (12, 10), (13, 9)))[way][kind]
        slots = 1 if kind == 2 else 2
        device = ((right, right, right2), (left, left, left2))[way][kind]
        return send(
            kv.at[pl.ds(at, slots), rows], kv.at[pl.ds(to, slots), rows],
            5 * PARTS + (kind * 2 + way) * PARTS + part, to * PARTS + part, device,
        )

    both_ways = [(part, way) for part in range(PARTS) for way in range(2)]
    for part, way in both_ways:
        for side in range(2):
            first_kv(way, part, side).start()
        if way == 1:
            pair_kv(part).start()
    loads[3].wait()
    sorted_q = nn_dot(order, q_ref[...]) * (HDIM ** -0.5)
    pq[...] = sorted_q.astype(BF16)
    for a in range(6):
        for part in range(2):
            q_sel[a // 3, 1 + 3 * part + a % 3] = picked(sorted_q, a, 4 * part)
    q_in[place, core] = q_sel[core]
    loads[4].start()

    pair_q = pltpu.make_async_remote_copy(
        q_sel.at[1 - core], q_in.at[place, core], pair_send.at[0], pair_recv.at[0],
        device_id=pair, device_id_type=MESH,
    )
    pair_q.start()

    def pass_on(stage):
        for part, way in both_ways:
            if stage == 0:
                for side in range(2):
                    first_arrival(way, part, side).wait_recv()
                passed(0, way, part).start()
            else:
                passed(0, way, part).wait_recv()
                passed(1, way, part).start()
                passed(2, way, part).start()

    def q_copy(i, side, inside):
        other, other_at, _ = partner(i)
        if inside:
            source, target, arrived = q_sel.at[side], q_in.at[place, core], q_recv_in.at[place, core]
        else:
            slot = out_slot(place, other_at)
            source, target = q_sel.at[side, pl.ds(0, 4)], q_out.at[slot, core]
            arrived = q_recv_out.at[slot, core]
        return pltpu.make_async_remote_copy(
            source, target, q_send.at[2 * i + side], arrived,
            device_id=(other, n - core + side), device_id_type=MESH,
        )

    def for_partners(act):
        @pl.loop(0, PARTNERS)
        def _(i):
            _, _, same = partner(i)

            @pl.when(same)
            def _():
                for side in range(2):
                    act(i, side, True)

            @pl.when(jnp.logical_not(same))
            def _():
                for side in range(2):
                    act(i, side, False)

    for_partners(lambda i, side, inside: q_copy(i, side, inside).start())

    ones = jnp.ones((TOK, 128), BF16)
    lane128 = lanes_of((TOK, 128))
    own_slide = jnp.where(lane128 < 16, (sorted_c - 1.0) * PENALTY, 0.0).astype(BF16)
    wide_low = lanes_of((TOK, 128)) < HDIM

    def local_pair(a):
        cols = slice(a * 128, (a + 1) * 128)
        block = pq[:, cols].astype(F32)
        left_side = jnp.concatenate(
            [
                jnp.concatenate([jnp.where(wide_low, block, 0.0).astype(BF16), own_slide], 1),
                jnp.concatenate([jnp.where(wide_low, 0.0, block).astype(BF16), own_slide], 1),
            ],
            0,
        )
        scores = nt_dot(left_side, jnp.concatenate([pk[:, cols], pc[...]], 1))
        top = jnp.max(scores, axis=1, keepdims=True)
        weights = jnp.exp(scores - top).astype(BF16)
        summed = nn_dot(weights, jnp.concatenate([pv[:, cols], ones], 1))
        result = summed[:, :128] / summed[:, 128:]
        level = top + jnp.log(summed[:, 128:])
        loc_o[:, cols] = jnp.where(wide_low, result[:TOK], result[TOK:])
        loc_l[:, cols] = jnp.where(wide_low, level[:TOK], level[TOK:])

    local_pair(0)
    local_pair(1)
    pass_on(0)
    local_pair(2)
    local_pair(3)
    pass_on(1)
    local_pair(4)
    local_pair(5)

    pair_q.wait_recv()

    @pl.loop(0, PARTNERS)
    def _(i):
        other, other_at, same = partner(i)

        @pl.when(same)
        def _():
            for side in range(2):
                spot = q_in.at[other_at, side]
                pltpu.make_async_copy(spot, spot, q_recv_in.at[other_at, side]).wait()

        @pl.when(jnp.logical_not(same))
        def _():
            slot = out_slot(other_at, place)
            for side in range(2):
                spot = q_out.at[slot, side]
                pltpu.make_async_copy(spot, spot, q_recv_out.at[slot, side]).wait()

    for side in range(2):
        for slot in range(SEG):
            q_roll[slot, side] = pltpu.roll(q_in[slot, side, 0].astype(F32), 64, 1).astype(BF16)

    def await_kv(parts):
        for part in parts:
            pair_kv_arrival(part).wait_recv()
            for way in range(2):
                passed(1, way, part).wait_recv()
                passed(2, way, part).wait_recv()

    many = jnp.ones((256, 128), BF16)
    half_masks = [
        jnp.where(low16, 1.0, 0.0).astype(BF16), jnp.where(low16, 0.0, 1.0).astype(BF16)
    ]
    masks = []
    for head in range(6):
        residue = lax.rem(6 * core + head, 8)
        masks.append(jnp.where(lane16 // 16 == residue, PENALTY, 0.0).astype(BF16))

    def stacked(value):
        return value.reshape(-1, 128)

    def left_side(block, slides, head):
        return jnp.concatenate(
            [stacked(block * half_masks[head % 2]), stacked((slides - 1) * masks[head])], 1
        )

    def levels(top, totals):
        return jnp.where(top < -PENALTY / 2, ABSENT, top + jnp.log(totals))

    def in_pieces(level):
        high = level.astype(BF16).astype(F32)
        rest = level - high
        middle = rest.astype(BF16).astype(F32)
        last = rest - middle
        at = lax.rem(lanes_of(level.shape), 8)
        pieces = jnp.where(
            at == 0, high, jnp.where(at == 1, middle, jnp.where(at == 2, last, 0.0))
        )
        return pieces.astype(BF16)

    def keys_of(part, j):
        slides = kv_roll[...] if part else kv[:, 0]
        return jnp.concatenate([stacked(kv[:, 1 + 6 * part + 2 * j]), stacked(slides)], 1)

    def values_of(part, j):
        return jnp.concatenate([stacked(kv[:, 2 + 6 * part + 2 * j]), many], 1)

    def inside(first, count):
        rows = count * 32
        span = pl.ds(first, count)
        low = lanes_of((rows, 128)) < HDIM
        spot = lanes_of((rows, 128)) // 8
        stats = jnp.zeros((rows, 128), F32)
        slides, turned = q_in[span, :, 0], q_roll[span]
        for j in range(3):
            far_q, near_q = q_in[span, :, 1 + j], q_in[span, :, 4 + j]
            lhs = jnp.concatenate(
                [
                    left_side(far_q, slides, 2 * j), left_side(near_q, turned, 2 * j),
                    left_side(far_q, slides, 2 * j + 1), left_side(near_q, turned, 2 * j + 1),
                ],
                0,
            )
            far_s, near_s = nt_dot(lhs, keys_of(0, j)), nt_dot(lhs, keys_of(1, j))
            top = jnp.max(jnp.maximum(far_s, near_s), axis=1, keepdims=True)
            far_o = nn_dot(jnp.exp(far_s - top).astype(BF16), values_of(0, j))
            both = far_o + nn_dot(jnp.exp(near_s - top).astype(BF16), values_of(1, j))
            for part in range(2):
                outs = []
                for u in range(2):
                    start = (2 * u + part) * rows
                    total = both[start:start + rows]
                    if part == 0:
                        total = total + far_o[start:start + rows]
                    outs.append(total[:, :128] / total[:, 128:])
                    level = levels(top[start:start + rows], total[:, 128:])
                    stats = jnp.where(spot == 8 * part + 2 * j + u, level, stats)
                o_in[span, :, 1 + 3 * part + j] = (
                    jnp.where(low, outs[0], outs[1]).astype(BF16).reshape(count, 2, 16, 128)
                )
        o_in[span, :, 0] = in_pieces(stats).reshape(count, 2, 16, 128)

    def outside(first, count):
        rows = count * 32
        span = pl.ds(first, count)
        low = lanes_of((rows, 128)) < HDIM
        spot = lanes_of((rows, 128)) // 8
        stats = jnp.zeros((rows, 128), F32)
        slides = q_out[span, :, 0]
        for j in range(3):
            far_q = q_out[span, :, 1 + j]
            lhs = jnp.concatenate(
                [left_side(far_q, slides, 2 * j), left_side(far_q, slides, 2 * j + 1)], 0
            )
            far_s = nt_dot(lhs, keys_of(0, j))
            top = jnp.max(far_s, axis=1, keepdims=True)
            total = nn_dot(jnp.exp(far_s - top).astype(BF16), values_of(0, j))
            result = total[:, :128] / total[:, 128:]
            level = levels(top, total[:, 128:])
            for u in range(2):
                stats = jnp.where(spot == 2 * j + u, level[u * rows:(u + 1) * rows], stats)
            o_out[span, :, 1 + j] = (
                jnp.where(low, result[:rows], result[rows:]).astype(BF16).reshape(count, 2, 16, 128)
            )
        o_out[span, :, 0] = in_pieces(stats).reshape(count, 2, 16, 128)

    def back_in(at, side):
        return pltpu.make_async_remote_copy(
            o_in.at[at, side], r_in.at[place, core], o_send_in.at[at, side],
            o_recv_in.at[place, core],
            device_id=(g - place + at, n - core + side), device_id_type=MESH,
        )

    def back_out(slot, side):
        at = lax.rem(slot + (place < 7).astype(jnp.int32) + place + 1, SEG)
        away = jnp.where(at > place, -SEG, SEG)
        other = lax.rem(g - place + at + away + WIDE, WIDE)
        return pltpu.make_async_remote_copy(
            o_out.at[slot, side], r_out.at[out_slot(place, at), core], o_send_out.at[slot, side],
            o_recv_out.at[out_slot(place, at), core],
            device_id=(other, n - core + side), device_id_type=MESH,
        )

    def if_near(at, act):
        apart = jnp.abs(at - place)

        @pl.when(jnp.logical_and(apart > 0, apart <= REACH))
        def _():
            for side in range(2):
                act(at, side)

    def if_used(slot, act):
        @pl.when(jnp.logical_or(slot < 5, lax.rem(place, 7) == 0))
        def _():
            for side in range(2):
                act(slot, side)

    await_kv((0, 1))

    outside(0, 6)

    @pl.loop(0, 6)
    def _(slot):
        if_used(slot, lambda slot, side: back_out(slot, side).start())

    for slot in range(16):
        kv_roll[slot] = pltpu.roll(kv[slot, 0].astype(F32), 64, 1).astype(BF16)
    await_kv((2, 3))

    @pl.loop(0, SEG // SLOTS)
    def _(step):
        chunk = lax.rem(step + place // SLOTS + 1, SEG // SLOTS)
        inside(SLOTS * chunk, SLOTS)
        for k in range(SLOTS):
            if_near(SLOTS * chunk + k, lambda at, side: back_in(at, side).start())

    pair_o = pltpu.make_async_remote_copy(
        o_in.at[place, 1 - core], r_in.at[place, core], pair_send.at[1], pair_recv.at[1],
        device_id=pair, device_id_type=MESH,
    )
    pair_o.start()
    r_in[place, core] = o_in[place, core]
    att[...] = loc_o[...]
    pair_q.wait_send()
    for part, way in both_ways:
        for side in range(2):
            first_kv(way, part, side).wait_send()
        if way == 1:
            pair_kv(part).wait_send()
        for kind in range(3):
            passed(kind, way, part).wait_send()
    for_partners(lambda i, side, inside: q_copy(i, side, inside).wait_send())

    pair_o.wait_send()

    @pl.loop(0, 6)
    def _(slot):
        if_used(slot, lambda slot, side: back_out(slot, side).wait_send())

    @pl.loop(0, SEG)
    def _(at):
        if_near(at, lambda at, side: back_in(at, side).wait_send())

    @pl.loop(0, PARTNERS)
    def _(i):
        other, other_at, same = partner(i)

        @pl.when(same)
        def _():
            for side in range(2):
                spot = r_in.at[other_at, side]
                pltpu.make_async_copy(spot, spot, o_recv_in.at[other_at, side]).wait()

        @pl.when(jnp.logical_not(same))
        def _():
            slot = out_slot(other_at, place)
            for side in range(2):
                spot = r_out.at[slot, side]
                pltpu.make_async_copy(spot, spot, o_recv_out.at[slot, side]).wait()

    pair_o.wait_recv()

    e_row = lax.broadcasted_iota(jnp.int32, (128, 384), 0)
    e_col = lax.broadcasted_iota(jnp.int32, (128, 384), 1)
    to_far = jnp.where((e_row // 8 == e_col // 64) & (e_row % 8 < 3), 1.0, 0.0).astype(BF16)
    to_near = jnp.where((e_row // 8 == e_col // 64 + 8) & (e_row % 8 < 3), 1.0, 0.0).astype(BF16)
    for half in range(2):
        stats_i = r_in[:, half, 0].reshape(128, 128)
        stats_o = r_out[:, half, 0].reshape(96, 128)
        far_i = nn_dot(stats_i, to_far)
        near_i = nn_dot(stats_i, to_near)
        far_o = nn_dot(stats_o, to_far)
        for j in range(3):
            a = 3 * half + j
            lanes = slice(j * 128, (j + 1) * 128)
            cols = slice(a * 128, (a + 1) * 128)
            for part in range(2):
                r0 = (2 * a + 4 * part) % 8 * 16
                r1 = r0 + 16
                own_l = jnp.where(low16, loc_l[r0:r0 + 16, cols], loc_l[r1:r1 + 16, cols])
                own_o = jnp.where(low16, loc_o[r0:r0 + 16, cols], loc_o[r1:r1 + 16, cols])
                lev = (near_i if part else far_i)[:, lanes].reshape(8, 16, 128)
                val = r_in[:, half, 1 + 3 * part + j].astype(F32)
                if part == 0:
                    lev = jnp.concatenate([lev, far_o[:, lanes].reshape(6, 16, 128)], 0)
                    val = jnp.concatenate([val, r_out[:, half, 1 + j].astype(F32)], 0)
                top = jnp.maximum(jnp.max(lev, axis=0), own_l)
                scale = jnp.exp(lev - top[None])
                own_scale = jnp.exp(own_l - top)
                numer = jnp.sum(scale * val, axis=0) + own_scale * own_o
                denom = jnp.sum(scale, axis=0) + own_scale
                joined = numer / denom
                att[r0:r0 + 16, a * 128:a * 128 + 64] = joined[:, :64]
                att[r1:r1 + 16, a * 128 + 64:a * 128 + 128] = joined[:, 64:]

    back = (row == 8 * (col % 16) + col // 16).astype(F32).astype(BF16)
    attended = nn_dot(back, att[...].astype(BF16)).astype(BF16)
    loads[4].wait()
    out_ref[...] = nn_dot(attended, w_vmem[...]).astype(BF16)


def local(queries, keys, values, slide_ids, w_out):
    vmem = pl.BlockSpec(memory_space=pltpu.VMEM)
    dma = pltpu.SemaphoreType.DMA
    return pl.pallas_call(
        kernel,
        out_shape=jax.ShapeDtypeStruct((TOK, WIDTH), BF16),
        in_specs=[pl.BlockSpec(memory_space=pltpu.HBM)] * 5,
        out_specs=vmem,
        scratch_shapes=[
            pltpu.VMEM((TOK, WIDTH), BF16),
            pltpu.VMEM((TOK, WIDTH), BF16),
            pltpu.VMEM((TOK, WIDTH), BF16),
            pltpu.VMEM((1, TOK), jnp.int32),
            pltpu.VMEM((TOK, WIDTH), BF16),
            pltpu.VMEM((TOK, WIDTH), BF16),
            pltpu.VMEM((TOK, WIDTH), BF16),
            pltpu.VMEM((TOK, 128), BF16),
            pltpu.VMEM((2, 13, 16, 128), BF16),
            pltpu.VMEM((2, 7, 16, 128), BF16),
            pltpu.VMEM((16, 13, 16, 128), BF16),
            pltpu.VMEM((16, 16, 128), BF16),
            pltpu.VMEM((8, 2, 7, 16, 128), BF16),
            pltpu.VMEM((6, 2, 4, 16, 128), BF16),
            pltpu.VMEM((8, 2, 16, 128), BF16),
            pltpu.VMEM((8, 2, 7, 16, 128), BF16),
            pltpu.VMEM((6, 2, 4, 16, 128), BF16),
            pltpu.VMEM((8, 2, 7, 16, 128), BF16),
            pltpu.VMEM((6, 2, 4, 16, 128), BF16),
            pltpu.VMEM((TOK, WIDTH), F32),
            pltpu.VMEM((TOK, WIDTH), F32),
            pltpu.VMEM((TOK, WIDTH), F32),
            pltpu.VMEM((WIDTH, WIDTH), BF16),
            dma((5,)),
            dma((2,)),
            dma((2,)),
            dma((11 * PARTS,)),
            dma((16 * PARTS,)),
            dma((24,)),
            dma((8, 2)),
            dma((6, 2)),
            dma((8, 2)),
            dma((6, 2)),
            dma((8, 2)),
            dma((6, 2)),
        ],
        compiler_params=pltpu.CompilerParams(
            collective_id=0, has_side_effects=True, vmem_limit_bytes=54960 * 1024
        ),
        name="dilated",
    )(queries, keys, values, slide_ids.reshape(1, TOK), w_out)


def solution(mesh):
    placed = (
        P(("wide", "narrow"), None),
        P(("wide", "narrow"), None),
        P(("wide", "narrow"), None),
        P(("wide", "narrow")),
        P(),
    )
    return jax.shard_map(
        local, mesh=mesh, in_specs=placed, out_specs=P(("wide", "narrow"), None), check_vma=False
    )
```

```python
import jax
import jax.numpy as jnp
from jax import lax
from jax.experimental import pallas as pl
from jax.experimental.pallas import tpu as pltpu
from jax.sharding import PartitionSpec as P

MESH = pl.DeviceIdType.MESH
HEADS = 12
HDIM = 64
WIDTH = 768
TOK = 128
WIDE = 32
SEG = 8
REACH = 6
PARTNERS = 2 * REACH
PENALTY = 2048.0
ABSENT = -1e30
BF16 = jnp.bfloat16
F32 = jnp.float32

KV_PARTS = ((0, 4), (4, 3), (7, 6))
PARTS = len(KV_PARTS)
SLOTS = 2


def lanes_of(shape):
    return lax.broadcasted_iota(jnp.int32, shape, len(shape) - 1)


def nt_dot(left, right):
    return lax.dot_general(left, right, (((1,), (1,)), ((), ())), preferred_element_type=F32)


def nn_dot(left, right):
    return lax.dot_general(left, right, (((1,), (0,)), ((), ())), preferred_element_type=F32)


def out_slot(sender_at, receiver_at):
    return lax.rem(sender_at - receiver_at + 15, 8) - (receiver_at < 7).astype(jnp.int32)


def kernel(
    q_hbm, k_hbm, v_hbm, ids_hbm, w_hbm, out_ref,
    q_ref, k_ref, v_ref, ids_ref,
    pq, pk, pv, pc, kv_sel, q_sel, kv, kv_roll, q_in, q_out, q_roll, o_in, o_out, r_in, r_out,
    loc_o, loc_l, att, w_vmem,
    in_sem, pair_send, pair_recv, ring_send, ring_recv,
    q_send, q_recv_in, q_recv_out, o_send_in, o_send_out, o_recv_in, o_recv_out,
):
    g = lax.axis_index("wide")
    n = lax.axis_index("narrow")
    place = lax.rem(g, SEG)
    core = lax.rem(n, 2)
    pair = (g, n + 1 - 2 * core)
    right = (g, lax.rem(n + 2, 16))
    left = (g, lax.rem(n + 14, 16))
    right2 = (g, lax.rem(n + 4, 16))
    left2 = (g, lax.rem(n + 12, 16))

    def partner(i):
        offset = i - REACH + (i >= REACH).astype(jnp.int32)
        other = lax.rem(g + offset + WIDE, WIDE)
        return other, lax.rem(other, SEG), other // SEG == g // SEG

    loads = [
        pltpu.make_async_copy(source, target, in_sem.at[at])
        for at, (source, target) in enumerate(
            ((ids_hbm, ids_ref), (k_hbm, k_ref), (v_hbm, v_ref), (q_hbm, q_ref), (w_hbm, w_vmem))
        )
    ]
    for load in loads[:4]:
        load.start()

    empty = jnp.where(lax.rem(lanes_of((2, 16, 128)), 8) == 0, ABSENT, 0.0).astype(BF16)
    spare = SEG - 1 - place
    r_in[spare] = jnp.zeros((2, 7, 16, 128), BF16)
    r_in[spare, :, 0] = empty
    r_out[5] = jnp.zeros((2, 4, 16, 128), BF16)
    r_out[5, :, 0] = empty

    barrier = pltpu.get_barrier_semaphore()
    turn = 1 - 2 * core
    crossed = ((g, right[1] + turn), (g, left[1] + turn))
    for device in (pair, right, left, right2, left2) + crossed:
        pl.semaphore_signal(barrier, inc=1, device_id=device, device_id_type=MESH)

    for apart in range(-REACH, REACH + 1):
        if apart:
            for side in range(2):
                pl.semaphore_signal(
                    barrier, inc=1, device_id_type=MESH,
                    device_id=(lax.rem(g + apart + WIDE, WIDE), n - core + side),
                )

    row = lax.broadcasted_iota(jnp.int32, (TOK, TOK), 0)
    col = lax.broadcasted_iota(jnp.int32, (TOK, TOK), 1)
    order = (col == 8 * (row % 16) + row // 16).astype(F32).astype(BF16)
    loads[0].wait()
    unlike = (jnp.broadcast_to(ids_ref[...], (TOK, TOK)) != row % 16).astype(F32).astype(BF16)
    sorted_c = nt_dot(order, unlike)
    pc[...] = sorted_c.astype(BF16)
    lane16 = lanes_of((16, 128))
    low16 = lane16 < HDIM
    others = jnp.zeros((16, 128), F32)
    for residue in range(8):
        others = jnp.where(
            lane16 // 16 == residue, sorted_c[residue * 16:residue * 16 + 16], others
        )
    others = others.astype(BF16)
    for half in range(2):
        kv_sel[half, 0] = others
        q_sel[half, 0] = others

    def picked(source, a, shift):
        first = (2 * a + shift) % 8
        block = source[:, a * 128:(a + 1) * 128]
        return jnp.where(
            low16, block[first * 16:first * 16 + 16], block[first * 16 + 16:first * 16 + 32]
        ).astype(BF16)

    loads[1].wait()
    sorted_k = nn_dot(order, k_ref[...])
    pk[...] = sorted_k.astype(BF16)
    for a in range(6):
        for part in range(2):
            kv_sel[a // 3, 1 + 2 * (a % 3) + 6 * part] = picked(sorted_k, a, 4 * part)
    loads[2].wait()
    sorted_v = nn_dot(order, v_ref[...])
    pv[...] = sorted_v.astype(BF16)
    for a in range(6):
        for part in range(2):
            kv_sel[a // 3, 2 + 2 * (a % 3) + 6 * part] = picked(sorted_v, a, 4 * part)
    kv[core] = kv_sel[core]
    pl.semaphore_wait(barrier, 7 + 2 * PARTNERS)

    def send(source, target, sent, arrived, device):
        return pltpu.make_async_remote_copy(
            source, target, ring_send.at[sent], ring_recv.at[arrived],
            device_id=device, device_id_type=MESH,
        )

    def pair_kv(part):
        first, count = KV_PARTS[part]
        rows = pl.ds(first, count)
        return send(
            kv_sel.at[1 - core, rows], kv.at[core, rows], part, core * PARTS + part, pair
        )

    def pair_kv_arrival(part):
        first, count = KV_PARTS[part]
        rows = pl.ds(first, count)
        other = 1 - core
        return send(kv_sel.at[core, rows], kv.at[other, rows], part, other * PARTS + part, pair)

    def first_kv(way, part, side):
        first, count = KV_PARTS[part]
        rows = pl.ds(first, count)
        slot = (2, 14)[way] + core
        device = (g, lax.rem(n - core + (2, 14)[way], 16) + side)
        return send(
            kv_sel.at[side, rows], kv.at[slot, rows],
            PARTS + (way * PARTS + part) * 2 + side, slot * PARTS + part, device,
        )

    def first_arrival(way, part, side):
        first, count = KV_PARTS[part]
        rows = pl.ds(first, count)
        slot = (2, 14)[way] + side
        return send(
            kv_sel.at[0, rows], kv.at[slot, rows],
            PARTS + (way * PARTS + part) * 2 + side, slot * PARTS + part, pair,
        )

    def passed(kind, way, part):
        first, count = KV_PARTS[part]
        rows = pl.ds(first, count)
        at, to = (((2, 4), (4, 6), (4, 8)), ((14, 12), (12, 10), (13, 9)))[way][kind]
        slots = 1 if kind == 2 else 2
        device = ((right, right, right2), (left, left, left2))[way][kind]
        return send(
            kv.at[pl.ds(at, slots), rows], kv.at[pl.ds(to, slots), rows],
            5 * PARTS + (kind * 2 + way) * PARTS + part, to * PARTS + part, device,
        )

    both_ways = [(part, way) for part in range(PARTS) for way in range(2)]
    for part, way in both_ways:
        for side in range(2):
            first_kv(way, part, side).start()
        if way == 1:
            pair_kv(part).start()
    loads[3].wait()
    sorted_q = nn_dot(order, q_ref[...]) * (HDIM ** -0.5)
    pq[...] = sorted_q.astype(BF16)
    for a in range(6):
        for part in range(2):
            q_sel[a // 3, 1 + 3 * part + a % 3] = picked(sorted_q, a, 4 * part)
    q_in[place, core] = q_sel[core]
    loads[4].start()

    pair_q = pltpu.make_async_remote_copy(
        q_sel.at[1 - core], q_in.at[place, core], pair_send.at[0], pair_recv.at[0],
        device_id=pair, device_id_type=MESH,
    )
    pair_q.start()

    def pass_on(stage):
        for part, way in both_ways:
            if stage == 0:
                for side in range(2):
                    first_arrival(way, part, side).wait_recv()
                passed(0, way, part).start()
            else:
                passed(0, way, part).wait_recv()
                passed(1, way, part).start()
                passed(2, way, part).start()

    def q_copy(i, side, inside):
        other, other_at, _ = partner(i)
        if inside:
            source, target, arrived = q_sel.at[side], q_in.at[place, core], q_recv_in.at[place, core]
        else:
            slot = out_slot(place, other_at)
            source, target = q_sel.at[side, pl.ds(0, 4)], q_out.at[slot, core]
            arrived = q_recv_out.at[slot, core]
        return pltpu.make_async_remote_copy(
            source, target, q_send.at[2 * i + side], arrived,
            device_id=(other, n - core + side), device_id_type=MESH,
        )

    def for_partners(act):
        @pl.loop(0, PARTNERS)
        def _(i):
            _, _, same = partner(i)

            @pl.when(same)
            def _():
                for side in range(2):
                    act(i, side, True)

            @pl.when(jnp.logical_not(same))
            def _():
                for side in range(2):
                    act(i, side, False)

    for_partners(lambda i, side, inside: q_copy(i, side, inside).start())

    ones = jnp.ones((TOK, 128), BF16)
    lane128 = lanes_of((TOK, 128))
    own_slide = jnp.where(lane128 < 16, (sorted_c - 1.0) * PENALTY, 0.0).astype(BF16)
    wide_low = lanes_of((TOK, 128)) < HDIM

    def local_pair(a):
        cols = slice(a * 128, (a + 1) * 128)
        block = pq[:, cols].astype(F32)
        left_side = jnp.concatenate(
            [
                jnp.concatenate([jnp.where(wide_low, block, 0.0).astype(BF16), own_slide], 1),
                jnp.concatenate([jnp.where(wide_low, 0.0, block).astype(BF16), own_slide], 1),
            ],
            0,
        )
        scores = nt_dot(left_side, jnp.concatenate([pk[:, cols], pc[...]], 1))
        top = jnp.max(scores, axis=1, keepdims=True)
        weights = jnp.exp(scores - top).astype(BF16)
        summed = nn_dot(weights, jnp.concatenate([pv[:, cols], ones], 1))
        result = summed[:, :128] / summed[:, 128:]
        level = top + jnp.log(summed[:, 128:])
        loc_o[:, cols] = jnp.where(wide_low, result[:TOK], result[TOK:])
        loc_l[:, cols] = jnp.where(wide_low, level[:TOK], level[TOK:])

    local_pair(0)
    local_pair(1)
    pass_on(0)
    local_pair(2)
    local_pair(3)
    pass_on(1)
    local_pair(4)
    local_pair(5)

    pair_q.wait_recv()

    @pl.loop(0, PARTNERS)
    def _(i):
        other, other_at, same = partner(i)

        @pl.when(same)
        def _():
            for side in range(2):
                spot = q_in.at[other_at, side]
                pltpu.make_async_copy(spot, spot, q_recv_in.at[other_at, side]).wait()

        @pl.when(jnp.logical_not(same))
        def _():
            slot = out_slot(other_at, place)
            for side in range(2):
                spot = q_out.at[slot, side]
                pltpu.make_async_copy(spot, spot, q_recv_out.at[slot, side]).wait()

    for side in range(2):
        for slot in range(SEG):
            q_roll[slot, side] = pltpu.roll(q_in[slot, side, 0].astype(F32), 64, 1).astype(BF16)

    def await_kv(parts):
        for part in parts:
            pair_kv_arrival(part).wait_recv()
            for way in range(2):
                passed(1, way, part).wait_recv()
                passed(2, way, part).wait_recv()

    many = jnp.ones((256, 128), BF16)
    half_masks = [
        jnp.where(low16, 1.0, 0.0).astype(BF16), jnp.where(low16, 0.0, 1.0).astype(BF16)
    ]
    masks = []
    for head in range(6):
        residue = lax.rem(6 * core + head, 8)
        masks.append(jnp.where(lane16 // 16 == residue, PENALTY, 0.0).astype(BF16))

    def stacked(value):
        return value.reshape(-1, 128)

    def left_side(block, slides, head):
        return jnp.concatenate(
            [stacked(block * half_masks[head % 2]), stacked((slides - 1) * masks[head])], 1
        )

    def levels(top, totals):
        return jnp.where(top < -PENALTY / 2, ABSENT, top + jnp.log(totals))

    def in_pieces(level):
        high = level.astype(BF16).astype(F32)
        rest = level - high
        middle = rest.astype(BF16).astype(F32)
        last = rest - middle
        at = lax.rem(lanes_of(level.shape), 8)
        pieces = jnp.where(
            at == 0, high, jnp.where(at == 1, middle, jnp.where(at == 2, last, 0.0))
        )
        return pieces.astype(BF16)

    def keys_of(part, j):
        slides = kv_roll[...] if part else kv[:, 0]
        return jnp.concatenate([stacked(kv[:, 1 + 6 * part + 2 * j]), stacked(slides)], 1)

    def values_of(part, j):
        return jnp.concatenate([stacked(kv[:, 2 + 6 * part + 2 * j]), many], 1)

    def inside(first, count):
        rows = count * 32
        span = pl.ds(first, count)
        low = lanes_of((rows, 128)) < HDIM
        spot = lanes_of((rows, 128)) // 8
        stats = jnp.zeros((rows, 128), F32)
        slides, turned = q_in[span, :, 0], q_roll[span]
        for j in range(3):
            far_q, near_q = q_in[span, :, 1 + j], q_in[span, :, 4 + j]
            lhs = jnp.concatenate(
                [
                    left_side(far_q, slides, 2 * j), left_side(near_q, turned, 2 * j),
                    left_side(far_q, slides, 2 * j + 1), left_side(near_q, turned, 2 * j + 1),
                ],
                0,
            )
            far_s, near_s = nt_dot(lhs, keys_of(0, j)), nt_dot(lhs, keys_of(1, j))
            top = jnp.max(jnp.maximum(far_s, near_s), axis=1, keepdims=True)
            far_o = nn_dot(jnp.exp(far_s - top).astype(BF16), values_of(0, j))
            both = far_o + nn_dot(jnp.exp(near_s - top).astype(BF16), values_of(1, j))
            for part in range(2):
                outs = []
                for u in range(2):
                    start = (2 * u + part) * rows
                    total = both[start:start + rows]
                    if part == 0:
                        total = total + far_o[start:start + rows]
                    outs.append(total[:, :128] / total[:, 128:])
                    level = levels(top[start:start + rows], total[:, 128:])
                    stats = jnp.where(spot == 8 * part + 2 * j + u, level, stats)
                o_in[span, :, 1 + 3 * part + j] = (
                    jnp.where(low, outs[0], outs[1]).astype(BF16).reshape(count, 2, 16, 128)
                )
        o_in[span, :, 0] = in_pieces(stats).reshape(count, 2, 16, 128)

    def outside(first, count):
        rows = count * 32
        span = pl.ds(first, count)
        low = lanes_of((rows, 128)) < HDIM
        spot = lanes_of((rows, 128)) // 8
        stats = jnp.zeros((rows, 128), F32)
        slides = q_out[span, :, 0]
        for j in range(3):
            far_q = q_out[span, :, 1 + j]
            lhs = jnp.concatenate(
                [left_side(far_q, slides, 2 * j), left_side(far_q, slides, 2 * j + 1)], 0
            )
            far_s = nt_dot(lhs, keys_of(0, j))
            top = jnp.max(far_s, axis=1, keepdims=True)
            total = nn_dot(jnp.exp(far_s - top).astype(BF16), values_of(0, j))
            result = total[:, :128] / total[:, 128:]
            level = levels(top, total[:, 128:])
            for u in range(2):
                stats = jnp.where(spot == 2 * j + u, level[u * rows:(u + 1) * rows], stats)
            o_out[span, :, 1 + j] = (
                jnp.where(low, result[:rows], result[rows:]).astype(BF16).reshape(count, 2, 16, 128)
            )
        o_out[span, :, 0] = in_pieces(stats).reshape(count, 2, 16, 128)

    def back_in(at, side):
        return pltpu.make_async_remote_copy(
            o_in.at[at, side], r_in.at[place, core], o_send_in.at[at, side],
            o_recv_in.at[place, core],
            device_id=(g - place + at, n - core + side), device_id_type=MESH,
        )

    def back_out(slot, side):
        at = lax.rem(slot + (place < 7).astype(jnp.int32) + place + 1, SEG)
        away = jnp.where(at > place, -SEG, SEG)
        other = lax.rem(g - place + at + away + WIDE, WIDE)
        return pltpu.make_async_remote_copy(
            o_out.at[slot, side], r_out.at[out_slot(place, at), core], o_send_out.at[slot, side],
            o_recv_out.at[out_slot(place, at), core],
            device_id=(other, n - core + side), device_id_type=MESH,
        )

    def if_near(at, act):
        apart = jnp.abs(at - place)

        @pl.when(jnp.logical_and(apart > 0, apart <= REACH))
        def _():
            for side in range(2):
                act(at, side)

    def if_used(slot, act):
        @pl.when(jnp.logical_or(slot < 5, lax.rem(place, 7) == 0))
        def _():
            for side in range(2):
                act(slot, side)

    await_kv((0, 1))

    outside(0, 6)

    @pl.loop(0, 6)
    def _(slot):
        if_used(slot, lambda slot, side: back_out(slot, side).start())

    for slot in range(16):
        kv_roll[slot] = pltpu.roll(kv[slot, 0].astype(F32), 64, 1).astype(BF16)
    await_kv((2,))

    @pl.loop(0, SEG // SLOTS)
    def _(step):
        chunk = lax.rem(step + place // SLOTS + 1, SEG // SLOTS)
        inside(SLOTS * chunk, SLOTS)
        for k in range(SLOTS):
            if_near(SLOTS * chunk + k, lambda at, side: back_in(at, side).start())

    pair_o = pltpu.make_async_remote_copy(
        o_in.at[place, 1 - core], r_in.at[place, core], pair_send.at[1], pair_recv.at[1],
        device_id=pair, device_id_type=MESH,
    )
    pair_o.start()
    r_in[place, core] = o_in[place, core]
    att[...] = loc_o[...]
    pair_q.wait_send()
    for part, way in both_ways:
        for side in range(2):
            first_kv(way, part, side).wait_send()
        if way == 1:
            pair_kv(part).wait_send()
        for kind in range(3):
            passed(kind, way, part).wait_send()
    for_partners(lambda i, side, inside: q_copy(i, side, inside).wait_send())

    pair_o.wait_send()

    @pl.loop(0, 6)
    def _(slot):
        if_used(slot, lambda slot, side: back_out(slot, side).wait_send())

    @pl.loop(0, SEG)
    def _(at):
        if_near(at, lambda at, side: back_in(at, side).wait_send())

    @pl.loop(0, PARTNERS)
    def _(i):
        other, other_at, same = partner(i)

        @pl.when(same)
        def _():
            for side in range(2):
                spot = r_in.at[other_at, side]
                pltpu.make_async_copy(spot, spot, o_recv_in.at[other_at, side]).wait()

        @pl.when(jnp.logical_not(same))
        def _():
            slot = out_slot(other_at, place)
            for side in range(2):
                spot = r_out.at[slot, side]
                pltpu.make_async_copy(spot, spot, o_recv_out.at[slot, side]).wait()

    pair_o.wait_recv()

    e_row = lax.broadcasted_iota(jnp.int32, (128, 384), 0)
    e_col = lax.broadcasted_iota(jnp.int32, (128, 384), 1)
    to_far = jnp.where((e_row // 8 == e_col // 64) & (e_row % 8 < 3), 1.0, 0.0).astype(BF16)
    to_near = jnp.where((e_row // 8 == e_col // 64 + 8) & (e_row % 8 < 3), 1.0, 0.0).astype(BF16)
    for half in range(2):
        stats_i = r_in[:, half, 0].reshape(128, 128)
        stats_o = r_out[:, half, 0].reshape(96, 128)
        far_i = nn_dot(stats_i, to_far)
        near_i = nn_dot(stats_i, to_near)
        far_o = nn_dot(stats_o, to_far)
        for j in range(3):
            a = 3 * half + j
            lanes = slice(j * 128, (j + 1) * 128)
            cols = slice(a * 128, (a + 1) * 128)
            for part in range(2):
                r0 = (2 * a + 4 * part) % 8 * 16
                r1 = r0 + 16
                own_l = jnp.where(low16, loc_l[r0:r0 + 16, cols], loc_l[r1:r1 + 16, cols])
                own_o = jnp.where(low16, loc_o[r0:r0 + 16, cols], loc_o[r1:r1 + 16, cols])
                lev = (near_i if part else far_i)[:, lanes].reshape(8, 16, 128)
                val = r_in[:, half, 1 + 3 * part + j].astype(F32)
                if part == 0:
                    lev = jnp.concatenate([lev, far_o[:, lanes].reshape(6, 16, 128)], 0)
                    val = jnp.concatenate([val, r_out[:, half, 1 + j].astype(F32)], 0)
                top = jnp.maximum(jnp.max(lev, axis=0), own_l)
                scale = jnp.exp(lev - top[None])
                own_scale = jnp.exp(own_l - top)
                numer = jnp.sum(scale * val, axis=0) + own_scale * own_o
                denom = jnp.sum(scale, axis=0) + own_scale
                joined = numer / denom
                att[r0:r0 + 16, a * 128:a * 128 + 64] = joined[:, :64]
                att[r1:r1 + 16, a * 128 + 64:a * 128 + 128] = joined[:, 64:]

    back = (row == 8 * (col % 16) + col // 16).astype(F32).astype(BF16)
    attended = nn_dot(back, att[...].astype(BF16)).astype(BF16)
    loads[4].wait()
    out_ref[...] = nn_dot(attended, w_vmem[...]).astype(BF16)


def local(queries, keys, values, slide_ids, w_out):
    vmem = pl.BlockSpec(memory_space=pltpu.VMEM)
    dma = pltpu.SemaphoreType.DMA
    return pl.pallas_call(
        kernel,
        out_shape=jax.ShapeDtypeStruct((TOK, WIDTH), BF16),
        in_specs=[pl.BlockSpec(memory_space=pltpu.HBM)] * 5,
        out_specs=vmem,
        scratch_shapes=[
            pltpu.VMEM((TOK, WIDTH), BF16),
            pltpu.VMEM((TOK, WIDTH), BF16),
            pltpu.VMEM((TOK, WIDTH), BF16),
            pltpu.VMEM((1, TOK), jnp.int32),
            pltpu.VMEM((TOK, WIDTH), BF16),
            pltpu.VMEM((TOK, WIDTH), BF16),
            pltpu.VMEM((TOK, WIDTH), BF16),
            pltpu.VMEM((TOK, 128), BF16),
            pltpu.VMEM((2, 13, 16, 128), BF16),
            pltpu.VMEM((2, 7, 16, 128), BF16),
            pltpu.VMEM((16, 13, 16, 128), BF16),
            pltpu.VMEM((16, 16, 128), BF16),
            pltpu.VMEM((8, 2, 7, 16, 128), BF16),
            pltpu.VMEM((6, 2, 4, 16, 128), BF16),
            pltpu.VMEM((8, 2, 16, 128), BF16),
            pltpu.VMEM((8, 2, 7, 16, 128), BF16),
            pltpu.VMEM((6, 2, 4, 16, 128), BF16),
            pltpu.VMEM((8, 2, 7, 16, 128), BF16),
            pltpu.VMEM((6, 2, 4, 16, 128), BF16),
            pltpu.VMEM((TOK, WIDTH), F32),
            pltpu.VMEM((TOK, WIDTH), F32),
            pltpu.VMEM((TOK, WIDTH), F32),
            pltpu.VMEM((WIDTH, WIDTH), BF16),
            dma((5,)),
            dma((2,)),
            dma((2,)),
            dma((11 * PARTS,)),
            dma((16 * PARTS,)),
            dma((24,)),
            dma((8, 2)),
            dma((6, 2)),
            dma((8, 2)),
            dma((6, 2)),
            dma((8, 2)),
            dma((6, 2)),
        ],
        compiler_params=pltpu.CompilerParams(
            collective_id=0, has_side_effects=True, vmem_limit_bytes=54960 * 1024
        ),
        name="dilated",
    )(queries, keys, values, slide_ids.reshape(1, TOK), w_out)


def solution(mesh):
    placed = (
        P(("wide", "narrow"), None),
        P(("wide", "narrow"), None),
        P(("wide", "narrow"), None),
        P(("wide", "narrow")),
        P(),
    )
    return jax.shard_map(
        local, mesh=mesh, in_specs=placed, out_specs=P(("wide", "narrow"), None), check_vma=False
    )
```
